256 devices in a mesh: band: 8 (over z), blk: 32 (over x, y, core).
Axes of the slice: x: 4, y: 4, z: 8, core: 2. Of those that a mesh axis runs over, the one named last changes fastest.
Arguments:
- ocean_state: bfloat16 [256, 960, 192], P('band', 'blk'), may hold values from -6 to 6
- ocean_mask: int32 [256, 960], P('band', 'blk'), may hold values 0 or 1
- cotangent: bfloat16 [256, 960, 192], P('band', 'blk'), may hold values from -6 to 6
- kernel: bfloat16 [7, 7, 192], replicated, may hold values from -0.875 to 0.875
- zonal_taps: bfloat16 [61, 192], replicated, may hold values from -0.75 to 0.75
- norm_gain: float32 [192], replicated, may hold values from 0.1 to 1.9
- weight_in: bfloat16 [192, 768], replicated, may hold values from -0.4375 to 0.4375
- weight_out: bfloat16 [768, 192], replicated, may hold values from -0.21875 to 0.21875
Outputs:
- grad_state: float32 [256, 960, 192], P('band', 'blk')
- grad_w_in: float32 [192, 768], replicated
- grad_w_out: float32 [768, 192], replicated
The draws below stay inside these ranges and needn't reach their ends.
Inputs may be any that keep to these rules, and one draw needn't show every extreme that they name: `ocean_mask`: 1 marks an ocean cell, 0 a land cell.
All inputs are finite; a program needn't handle non-finite values. No bound on the sum of `ocean_mask` on one device may be relied on, other than what follows from the above.
Results may differ from the reference program's by a relative error of at most 0.018.
Values may be sent and summed in bfloat16 or wider, within the bound.
No kernel may reach another device: no remote copies, remote signals or barrier semaphores. Data moves between devices by JAX's collectives and lax.ppermute only.
A program may use at most 128 MiB of HBM per device.

```python
import math
import jax
import jax.numpy as jnp
from jax import lax

C = 192
HID = 768
KSIZE = 7
TAPS = 61
STEPS = 2
RIM = 3
HALF = 30
NY = 256
NX = 960


def plant(array, rng, low, high):
    place = [jax.random.randint(jax.random.fold_in(rng, axis), (), 0, length) for axis, length in enumerate(array.shape)]
    widest = array.shape.index(max(array.shape))
    neighbour = place[:widest] + [(place[widest] + 1) % array.shape[widest]] + place[widest + 1:]
    return array.at[tuple(place)].set(low).at[tuple(neighbour)].set(high)


def levels(own_key, extent, pieces, smallest, high):
    level = 1.0
    for position, parts in pieces:
        draws = jax.random.uniform(jax.random.fold_in(jax.random.fold_in(own_key, 6), position), (parts,), jnp.float32, smallest / len(pieces), high / len(pieces))
        level = level * jnp.repeat(jnp.exp(draws), extent[position] // parts).reshape((-1,) + (1,) * (len(extent) - 1 - position))
    return level


def noise(stream_key, extent, deviation, bound, shards=(), dtype=jnp.bfloat16):
    values = jax.random.normal(stream_key, extent, jnp.float32) * deviation
    if len(shards) > 0:
        values = levels(stream_key, extent, shards, -0.22, 0.18) * values
    return jnp.clip(values, min=-bound, max=bound).astype(dtype)


def setup_inputs(seed: int = 0) -> dict:
    arg_keys = jax.random.split(jax.random.key(seed), 9)
    ocean_state = noise(arg_keys[0], (NY, NX, C), 1.0, 6.0, ((0, 8), (1, 32)))
    ocean_mask = plant((jax.random.randint(arg_keys[1], (NY, NX), 0, 4) < 3).astype(jnp.int32), jax.random.fold_in(arg_keys[1], 1), 0, 1)
    cotangent = noise(arg_keys[2], (NY, NX, C), 1.0, 6.0, ((0, 8), (1, 32)))
    kernel = noise(arg_keys[3], (KSIZE, KSIZE, C), (KSIZE * KSIZE) ** -0.5, 0.875)
    zonal_taps = noise(arg_keys[4], (TAPS, C), TAPS ** -0.5, 0.75)
    norm_gain = jnp.clip(1.0 + 0.18 * jax.random.normal(arg_keys[5], (C,), jnp.float32), 0.1, 1.9)
    weight_in = noise(arg_keys[6], (C, HID), C ** -0.5, 0.4375)
    weight_out = noise(arg_keys[7], (HID, C), HID ** -0.5, 0.21875)
    return dict(ocean_state=ocean_state, ocean_mask=ocean_mask, cotangent=cotangent, kernel=kernel, zonal_taps=zonal_taps, norm_gain=norm_gain, weight_in=weight_in, weight_out=weight_out)


epsilon = 1e-06
conv_layout = ('NHWC', 'HWIO', 'NHWC')

def depthwise(values, kernel):
    result = lax.conv_general_dilated(values[None], kernel[:, :, None, :], (1, 1), 'VALID', dimension_numbers=conv_layout, feature_group_count=values.shape[2], preferred_element_type=jnp.float32)
    return result[0]

def wrap_columns(values, margin):
    return jnp.concatenate([values[:, -margin:], values, values[:, :margin]], axis=1)

def extend_whole(values):
    north_rows = values[-RIM:][::-1, ::-1]
    south_rows = jnp.zeros_like(values[:RIM])
    stacked = jnp.concatenate([south_rows, values, north_rows], axis=0)
    return wrap_columns(stacked, RIM)

def extend_adjoint(grad_ext):
    interior = grad_ext[:, RIM:-RIM]
    interior = interior.at[:, -RIM:].add(grad_ext[:, :RIM])
    interior = interior.at[:, :RIM].add(grad_ext[:, -RIM:])
    result = interior[RIM:-RIM]
    return result.at[-RIM:].add(interior[-RIM:][::-1, ::-1])

def normalize(mixture, norm_gain):
    average = lax.optimization_barrier(jnp.mean(mixture, axis=-1, keepdims=True))
    centered = mixture - average
    variance = lax.optimization_barrier(jnp.mean(centered * centered, axis=-1, keepdims=True))
    return centered * lax.rsqrt(variance + epsilon) * norm_gain

def flat_dot(left_side, right_side):
    product = jnp.dot(left_side.reshape(-1, left_side.shape[-1]), right_side, preferred_element_type=jnp.float32)
    return product.reshape(left_side.shape[:-1] + (right_side.shape[-1],))

def mix_forward(current, kernel, zonal_taps):
    local_mix = depthwise(extend_whole(current), kernel)
    zonal = depthwise(wrap_columns(current, HALF), zonal_taps[None]).astype(jnp.bfloat16)
    return local_mix + zonal.astype(jnp.float32)

def mlp_parts(mixture, norm_gain, weight_in):
    normed = normalize(mixture, norm_gain).astype(jnp.bfloat16)
    preact = flat_dot(normed, weight_in)
    hidden = jax.nn.gelu(preact).astype(jnp.bfloat16)
    return (normed, preact, hidden)

def step_backward(current, ocean_weight, adjoint, kernel, zonal_taps, norm_gain, weight_in, weight_out):
    mixture = mix_forward(current, kernel, zonal_taps)
    normed, preact, hidden = mlp_parts(mixture, norm_gain, weight_in)
    grad_update = (ocean_weight * adjoint).astype(jnp.bfloat16)
    grad_out = jnp.dot(hidden.reshape(-1, HID).T, grad_update.reshape(-1, C), preferred_element_type=jnp.float32)
    grad_hidden = flat_dot(grad_update, weight_out.T)
    gelu_back = jax.vjp(jax.nn.gelu, preact)[1]
    grad_preact = gelu_back(grad_hidden)[0].astype(jnp.bfloat16)
    grad_in = jnp.dot(normed.reshape(-1, C).T, grad_preact.reshape(-1, HID), preferred_element_type=jnp.float32)
    grad_normed = flat_dot(grad_preact, weight_in.T)
    norm_back = jax.vjp(lambda mixed_in: normalize(mixed_in, norm_gain), mixture)[1]
    grad_mixed = norm_back(grad_normed)[0].astype(jnp.bfloat16)
    padded = jnp.pad(grad_mixed, ((KSIZE - 1, KSIZE - 1), (KSIZE - 1, KSIZE - 1), (0, 0)))
    grad_local = extend_adjoint(depthwise(padded, kernel[::-1, ::-1]))
    grad_zonal = depthwise(wrap_columns(grad_mixed, HALF), zonal_taps[::-1][None]).astype(jnp.bfloat16)
    updated = ocean_weight * adjoint + grad_local + grad_zonal.astype(jnp.float32)
    return (updated, grad_in, grad_out)

def reference(ocean_state, ocean_mask, cotangent, kernel, zonal_taps, norm_gain, weight_in, weight_out):
    ocean_weight = ocean_mask[:, :, None].astype(jnp.float32)
    states = [ocean_state]
    for section_index in range(STEPS):
        current = states[-1]
        mixture = mix_forward(current, kernel, zonal_taps)
        normed, preact, hidden = mlp_parts(mixture, norm_gain, weight_in)
        update = flat_dot(hidden, weight_out)
        states.append((ocean_weight * (current.astype(jnp.float32) + update)).astype(jnp.bfloat16))
    adjoint = cotangent.astype(jnp.float32)
    total_in = jnp.zeros(weight_in.shape, jnp.float32)
    total_out = jnp.zeros(weight_out.shape, jnp.float32)
    for section_index in range(STEPS - 1, -1, -1):
        adjoint, grad_in, grad_out = step_backward(states[section_index], ocean_weight, adjoint, kernel, zonal_taps, norm_gain, weight_in, weight_out)
        total_in = total_in + grad_in
        total_out = total_out + grad_out
    scaling = 1.0 / math.sqrt(NY * NX)
    return (adjoint, total_in * scaling, total_out * scaling)
```

```python
import math

import jax
import jax.numpy as jnp
from jax import lax
from jax.sharding import PartitionSpec as P

STEPS = 2


epsilon = 1e-06
conv_layout = ("NHWC", "HWIO", "NHWC")


def with_halo(block, sides, width, periodic):
    for axis, dim in sides:
        count = lax.axis_size(axis)
        forward = [(i, i + 1) for i in range(count - 1)]
        if periodic:
            forward.append((count - 1, 0))
        backward = [(target, source) for source, target in forward]
        low = lax.ppermute(
            lax.slice_in_dim(block, block.shape[dim] - width, None, axis=dim), axis, forward
        )
        high = lax.ppermute(lax.slice_in_dim(block, 0, width, axis=dim), axis, backward)
        block = jnp.concatenate([low, block, high], axis=dim)
    return block


def depthwise(values, kernel):
    result = lax.conv_general_dilated(
        values[None],
        kernel[:, :, None, :],
        (1, 1),
        "VALID",
        dimension_numbers=conv_layout,
        feature_group_count=values.shape[2],
        preferred_element_type=jnp.float32,
    )
    return result[0]


def normalize(mixture, norm_gain):
    average = jnp.mean(mixture, axis=-1, keepdims=True)
    centered = mixture - average
    variance = jnp.mean(centered * centered, axis=-1, keepdims=True)
    return centered * lax.rsqrt(variance + epsilon) * norm_gain


def flat_dot(left_side, right_side):
    product = jnp.dot(
        left_side.reshape(-1, left_side.shape[-1]), right_side, preferred_element_type=jnp.float32
    )
    return product.reshape(left_side.shape[:-1] + (right_side.shape[-1],))


def mlp_parts(mixture, norm_gain, weight_in):
    normed = normalize(mixture, norm_gain).astype(jnp.bfloat16)
    preact = flat_dot(normed, weight_in)
    hidden = jax.nn.gelu(preact).astype(jnp.bfloat16)
    return (normed, preact, hidden)


def mirrored(rows):
    bands, blocks = lax.axis_size("band"), lax.axis_size("blk")
    first = (bands - 1) * blocks
    pairs = [(first + i, first + blocks - 1 - i) for i in range(blocks)]
    return lax.ppermute(rows, ("band", "blk"), pairs)


def ways(axis, low, count):
    position = (lax.axis_index(axis) // low) % count
    pairs = [
        [(i, i ^ (low * step)) for i in range(lax.axis_size(axis))] for step in range(count)
    ]
    return position, pairs


def scattered_sum(parts, axis, low, count):
    position, pairs = ways(axis, low, count)
    parts = parts.reshape((count, -1) + parts.shape[1:])
    total = lax.dynamic_index_in_dim(parts, position, 0, False)
    arrived = []
    for step in range(1, count):
        piece = lax.dynamic_index_in_dim(parts, position ^ step, 0, False).astype(jnp.bfloat16)
        arrived.append(lax.ppermute(piece, axis, pairs[step]))
    for piece in arrived:
        total = total + piece.astype(jnp.float32)
    return total


def gathered(value, axis, low, count):
    position, pairs = ways(axis, low, count)
    whole = jnp.zeros((count,) + value.shape, value.dtype)
    whole = lax.dynamic_update_index_in_dim(whole, value, position, 0)
    for step in range(1, count):
        piece = lax.ppermute(value, axis, pairs[step])
        whole = lax.dynamic_update_index_in_dim(whole, piece, position ^ step, 0)
    return whole.reshape((-1,) + value.shape[1:])


def summed(value):
    stages = (("blk", 1, 2), ("blk", 2, 4), ("blk", 8, 4))
    for stage in stages:
        value = scattered_sum(value, *stage)
    terms = gathered(value.astype(jnp.bfloat16)[None], "band", 1, 8)
    value = jnp.sum(terms.astype(jnp.float32), axis=0).astype(jnp.bfloat16)
    for stage in stages[::-1]:
        value = gathered(value, *stage)
    return value.astype(jnp.float32)


def filters(values, north_rows, rim, zonal_taps):
    row_count = values.shape[0]
    margin = zonal_taps.shape[0] // 2
    widened = with_halo(values, (("band", 0),), rim, False)
    widened = jnp.concatenate(
        [widened[: row_count + rim], widened[row_count + rim :] + north_rows], axis=0
    )
    spread = with_halo(widened, (("blk", 1),), rim, True)
    wide = with_halo(values, (("blk", 1),), margin, True)
    zonal = depthwise(wide, zonal_taps[None]).astype(jnp.bfloat16)
    return (spread, zonal)


def shards(
    ocean_state, ocean_mask, cotangent, kernel, zonal_taps, norm_gain, weight_in, weight_out
):
    rim = kernel.shape[0] // 2
    row_count = ocean_state.shape[0]
    channels = ocean_state.shape[2]
    hidden_units = weight_in.shape[1]
    ocean_weight = ocean_mask[:, :, None].astype(jnp.float32)
    no_rows = jnp.zeros((rim,) + ocean_state.shape[1:], jnp.bfloat16)
    states = [ocean_state]
    mixtures = []
    for section_index in range(STEPS):
        current = states[-1]
        north_rows = mirrored(current[-rim:][::-1, ::-1])
        spread, zonal = filters(current, north_rows, rim, zonal_taps)
        mixture = depthwise(spread, kernel) + zonal.astype(jnp.float32)
        normed, preact, hidden = mlp_parts(mixture, norm_gain, weight_in)
        update = flat_dot(hidden, weight_out)
        mixtures.append(mixture)
        states.append((ocean_weight * (current.astype(jnp.float32) + update)).astype(jnp.bfloat16))
    adjoint = cotangent.astype(jnp.float32)
    total_in = jnp.zeros(weight_in.shape, jnp.float32)
    total_out = jnp.zeros(weight_in.shape, jnp.float32)
    for section_index in range(STEPS - 1, -1, -1):
        mixture = mixtures[section_index]
        normed, preact, hidden = mlp_parts(mixture, norm_gain, weight_in)
        grad_update = (ocean_weight * adjoint).astype(jnp.bfloat16)
        total_out = total_out + jnp.dot(
            grad_update.reshape(-1, channels).T,
            hidden.reshape(-1, hidden_units),
            preferred_element_type=jnp.float32,
        )
        grad_hidden = flat_dot(grad_update, weight_out.T)
        gelu_back = jax.vjp(jax.nn.gelu, preact)[1]
        grad_preact = gelu_back(grad_hidden)[0].astype(jnp.bfloat16)
        total_in = total_in + jnp.dot(
            normed.reshape(-1, channels).T,
            grad_preact.reshape(-1, hidden_units),
            preferred_element_type=jnp.float32,
        )
        grad_normed = flat_dot(grad_preact, weight_in.T)
        norm_back = jax.vjp(lambda mixed_in: normalize(mixed_in, norm_gain), mixture)[1]
        grad_mixed = norm_back(grad_normed)[0].astype(jnp.bfloat16)
        spread, grad_zonal = filters(grad_mixed, no_rows, rim, zonal_taps[::-1])
        padded = jnp.pad(spread, ((0, rim), (0, 0), (0, 0)))
        transposed = depthwise(padded, kernel[::-1, ::-1])
        ghost_grads = transposed[row_count:]
        returned = mirrored(ghost_grads[::-1, ::-1].astype(jnp.bfloat16)).astype(jnp.float32)
        placed = jnp.pad(returned, ((row_count - rim, 0), (0, 0), (0, 0)))
        grad_local = transposed[:row_count] + placed
        adjoint = ocean_weight * adjoint + grad_local + grad_zonal.astype(jnp.float32)
    terms = jnp.concatenate([total_in, total_out]).reshape(2 * channels, -1, 128)
    terms = summed(terms.swapaxes(0, 1).reshape(-1, 128))
    terms = terms.reshape(-1, 2 * channels, 128).swapaxes(0, 1).reshape(2 * channels, -1)
    summed_in, summed_out = terms[:channels], terms[channels:].T
    cell_count = row_count * lax.axis_size("band") * ocean_state.shape[1] * lax.axis_size("blk")
    scaling = 1.0 / math.sqrt(cell_count)
    return (adjoint, summed_in * scaling, summed_out * scaling)


def solution(mesh):
    return jax.shard_map(
        shards,
        mesh=mesh,
        in_specs=(
            P("band", "blk", None),
            P("band", "blk"),
            P("band", "blk", None),
            P(),
            P(),
            P(),
            P(),
            P(),
        ),
        out_specs=(P("band", "blk", None), P(), P()),
        check_vma=False,
    )
```

```python
import functools
import math

import jax
import jax.numpy as jnp
import numpy as np
from jax import lax
from jax.experimental import pallas as pl
from jax.experimental.pallas import tpu as pltpu
from jax.sharding import PartitionSpec as P

ROWS, COLS, CHANNELS, HIDDEN = 32, 30, 192, 768
WIDE = 32
CELLS = ROWS * WIDE
RIM, HALF, GROUP, GROUPS, PLACES = 3, 30, 64, 3, 4
ZONAL_TILES, LOCAL_TILES = 24, 21
TILE = GROUP * PLACES
CHUNK = 256
bf16, f32 = jnp.bfloat16, jnp.float32
epsilon = 1e-06
gelu_scale, gelu_cube = math.sqrt(2.0 / math.pi), 0.044715


def ways(axis, low, count):
    position = (lax.axis_index(axis) // low) % count
    pairs = [
        [(i, i ^ (low * step)) for i in range(lax.axis_size(axis))] for step in range(count)
    ]
    return position, pairs


def scattered_sum(parts, axis, low, count):
    position, pairs = ways(axis, low, count)
    parts = parts.reshape((count, -1) + parts.shape[1:])
    total = lax.dynamic_index_in_dim(parts, position, 0, False)
    arrived = []
    for step in range(1, count):
        piece = lax.dynamic_index_in_dim(parts, position ^ step, 0, False).astype(bf16)
        arrived.append(lax.ppermute(piece, axis, pairs[step]))
    for piece in arrived:
        total = total + piece.astype(f32)
    return total


def gathered(value, axis, low, count):
    position, pairs = ways(axis, low, count)
    whole = jnp.zeros((count,) + value.shape, value.dtype)
    whole = lax.dynamic_update_index_in_dim(whole, value, position, 0)
    for step in range(1, count):
        piece = lax.ppermute(value, axis, pairs[step])
        whole = lax.dynamic_update_index_in_dim(whole, piece, position ^ step, 0)
    return whole


def summed(value):
    value = scattered_sum(value, "blk", 1, 2)
    value = scattered_sum(value, "blk", 2, 4)
    for stage in (("blk", 8, 4), ("band", 1, 4), ("band", 4, 2)):
        value = jnp.sum(gathered(value.astype(bf16), *stage).astype(f32), axis=0)
    value = gathered(value.astype(bf16), "blk", 2, 4).reshape(-1, 128)
    return gathered(value, "blk", 1, 2).reshape(-1, 128)


def halos(packed, edge_rows):
    bands, blocks = lax.axis_size("band"), lax.axis_size("blk")
    band, block = lax.axis_index("band"), lax.axis_index("blk")
    odd_band, odd_block = band % 2 == 1, block % 2 == 1
    inner = [(i, i ^ 1) for i in range(blocks)]
    outer = [(i, (i + 1) % blocks if i % 2 else (i - 1) % blocks) for i in range(blocks)]
    near = [
        (b * blocks + i, (b ^ 1) * blocks + i) for b in range(bands) for i in range(blocks)
    ]
    far = [
        (b * blocks + i, (b + 1 if b % 2 else b - 1) * blocks + i)
        for b in range(1, bands - 1)
        for i in range(blocks)
    ]
    last = (bands - 1) * blocks
    far += [(last + i, last + blocks - 1 - i) for i in range(blocks)]
    low, high = edge_rows[0], edge_rows[1]
    turned = jnp.pad(high[::-1, :COLS][:, ::-1], ((0, 0), (0, WIDE - COLS), (0, 0)))
    to_far = jnp.where(odd_band, jnp.where(band == bands - 1, turned, high), low)
    outer_block = lax.ppermute(packed, "blk", outer)
    far_rows = lax.ppermute(to_far, ("band", "blk"), far)
    near_rows = lax.ppermute(jnp.where(odd_band, low, high), ("band", "blk"), near)
    inner_block = lax.ppermute(packed, "blk", inner)
    south = jnp.where(odd_band, near_rows, far_rows)
    north = jnp.where(odd_band, far_rows, near_rows)
    rows = jnp.concatenate([south, north])
    first, final = rows[:, :RIM], rows[:, COLS - RIM : COLS]
    outer_corner = lax.ppermute(jnp.where(odd_block, final, first), "blk", outer)
    inner_corner = lax.ppermute(jnp.where(odd_block, first, final), "blk", inner)
    west = jnp.where(odd_block, inner_corner, outer_corner)
    east = jnp.where(odd_block, outer_corner, inner_corner)
    rim_rows = jnp.concatenate(
        [west, rows[:, :COLS], east, jnp.zeros((2 * RIM, 4, CHANNELS), bf16)], axis=1
    )
    return inner_block, outer_block, rim_rows


def zonal_entries(taps):
    padded = jnp.pad(taps.astype(f32), ((24, 96 + 24 - taps.shape[0]), (0, 0)))
    eights = padded.reshape(-1, 8, GROUPS, GROUP)
    index = np.array(
        [[[4 * m + i - o + 3 for o in range(PLACES)] for i in range(PLACES)] for m in range(3)]
    )
    picked = jnp.stack([eights[k] for k in index.reshape(-1)])
    picked = picked.reshape(3, PLACES, PLACES, 8, GROUPS, GROUP)
    return picked.transpose(4, 0, 3, 1, 2, 5).reshape(GROUPS, 96, TILE)


def local_entries(kernel):
    size = kernel.shape[0]
    padded = jnp.pad(kernel.astype(f32), ((4, 4), (0, 0), (0, 0)))
    picked = jnp.stack(
        [
            padded[4 * (b - 1) + i - o + RIM + 4]
            for b in range(3)
            for i in range(PLACES)
            for o in range(PLACES)
        ]
    )
    picked = picked.reshape(3, PLACES, PLACES, size, GROUPS, GROUP)
    return picked.transpose(4, 0, 3, 1, 2, 5).reshape(GROUPS, 3 * size * PLACES, TILE)


def low_lanes(shape):
    return lax.broadcasted_iota(jnp.int32, shape, len(shape) - 1) < GROUP


def swap_halves(value):
    return pltpu.roll(value, GROUP, value.ndim - 1)


def mix(
    parity, own, inner, outer, rim_rows, zonal_v, local_v, north_v, scratch
):
    wide, pairs, rim, row_pairs, zonal_left, local_left, right, zonal_out, local_out = scratch
    odd = parity[0] == 1
    for r in range(48):
        ins, outs = inner[r].astype(f32), outer[r].astype(f32)
        wide[r, 96:112] = jnp.zeros((16, 128), f32)
        wide[r, 88:96] = jnp.zeros((8, 128), f32)
        wide[r, 0:8] = jnp.zeros((8, 128), f32)
        wide[r, 2:34] = jnp.where(odd, ins, outs)
        wide[r, 32:64] = own[r].astype(f32)
        wide[r, 62:94] = jnp.where(odd, outs, ins)
    low = low_lanes((104, 128))
    for r in range(ROWS):
        value = wide[r]
        turned = swap_halves(value)
        pairs[0, r] = jnp.where(low, value[:104], turned[8:])
        pairs[1, r] = jnp.where(low, turned[:104], value[8:])
    for r in range(16):
        value = wide[32 + r]
        turned = swap_halves(value)
        pairs[2, r] = jnp.where(low, value[:104], turned[8:])
        pairs[2, 16 + r] = jnp.where(low, turned[:104], value[8:])
    for k in range(2 * RIM):
        value = rim_rows[k].astype(f32)
        rim[0, k, 0:8] = jnp.zeros((8, 128), f32)
        rim[1, k, 0:8] = jnp.zeros((8, 128), f32)
        rim[0, k, 5:45] = value[:, :128]
        rim[1, k, 5:45, 0:GROUP] = value[:, 128:]
        rim[1, k, 5:45, GROUP:] = jnp.zeros((40, GROUP), f32)
    low = low_lanes((40, 128))
    nothing = jnp.zeros((40, 128), f32)

    def at(part, row):
        if row < -RIM or row >= ROWS + RIM:
            return nothing
        if row < 0:
            return rim[part, row + RIM, 0:40]
        if row >= ROWS:
            return rim[part, row - ROWS + RIM, 0:40]
        return wide[row, 24:64] if part == 0 else wide[32 + row % 16, 24:64]

    def columns(part, row):
        if 0 <= row < ROWS:
            return wide[row, 24:72] if part == 0 else wide[32 + row % 16, 24:72]
        if row < -RIM or row >= ROWS + RIM:
            return jnp.zeros((48, 128), f32)
        k = row + RIM if row < 0 else row - ROWS + RIM
        return jnp.concatenate([rim[part, k, 0:40], rim[part, k, 40:48]])

    low = low_lanes((48, 128))
    for q in range(20):
        first, second = columns(0, 2 * q - 4), columns(0, 2 * q - 3)
        row_pairs[0, q] = jnp.where(low, first, swap_halves(second))
        row_pairs[1, q] = jnp.where(low, swap_halves(first), second)
        first, second = columns(1, 2 * q - 4), columns(1, 2 * q - 3)
        if 16 <= 2 * q - 4 < ROWS:
            row_pairs[2, q] = jnp.where(low, swap_halves(first), second)
        else:
            row_pairs[2, q] = jnp.where(low, first, swap_halves(second))
    unit = (
        lax.broadcasted_iota(jnp.int32, (GROUP, TILE), 0)
        == lax.broadcasted_iota(jnp.int32, (GROUP, TILE), 1) % GROUP
    )
    unit = jnp.where(unit, 1.0, 0.0).astype(bf16)

    def spread(entries, g, index):
        row = jnp.broadcast_to(entries[g, index : index + 1, :], (16, TILE)).astype(bf16)
        return jnp.concatenate([row] * (GROUP // 16)) * unit

    @pl.loop(0, GROUPS)
    def _(g):
        for tile in range(ZONAL_TILES):
            start = 2 + tile % 8 + 32 * (tile // 8)
            first = pairs[g, :, start : start + 8, :].reshape(CHUNK, 128)
            second = pairs[g, :, start + 16 : start + 24, :].reshape(CHUNK, 128)
            zonal_left[:, tile * TILE : tile * TILE + 128] = first.astype(bf16)
            zonal_left[:, tile * TILE + 128 : (tile + 1) * TILE] = second.astype(bf16)
        for k in range(ZONAL_TILES * PLACES):
            right[k * GROUP : (k + 1) * GROUP] = spread(zonal_v, g, k)
        zonal_out[g] = jnp.dot(
            zonal_left[...], right[: ZONAL_TILES * TILE], preferred_element_type=f32
        )
        for shift in range(7):
            for half in range(2):
                for block in range(10):
                    value = row_pairs[g, 2 * block + half, 5 + shift : 37 + shift, :]
                    local_left[
                        block * 32 : block * 32 + 32,
                        shift * TILE + half * 128 : shift * TILE + half * 128 + 128,
                    ] = value.astype(bf16)
        for k in range(LOCAL_TILES * PLACES):
            right[k * GROUP : (k + 1) * GROUP] = spread(local_v, g, k)
        for k in range(7 * PLACES):
            place = LOCAL_TILES * PLACES + k
            right[place * GROUP : (place + 1) * GROUP] = spread(north_v, g, k)
        depth = 7 * TILE
        total = jnp.dot(local_left[0:256], right[0:depth], preferred_element_type=f32)
        total += jnp.dot(
            local_left[32:288], right[depth : 2 * depth], preferred_element_type=f32
        )
        local_out[g] = total
        local_out[g, 0:224] += jnp.dot(
            local_left[64:288], right[2 * depth : 3 * depth], preferred_element_type=f32
        )
        local_out[g, 224:256] += jnp.dot(
            local_left[288:320], right[3 * depth : 4 * depth], preferred_element_type=f32
        )


def mixed_rows(row, zonal_out, local_out):
    low = low_lanes((8, 128))
    block, place = row // PLACES, row % PLACES

    def joined(first, second, third, odd):
        mask = low_lanes(first.shape)
        if odd:
            return jnp.where(mask, swap_halves(first), second), swap_halves(third)
        return jnp.where(mask, first, swap_halves(second)), third

    lanes = slice(place // 2 * 128, place // 2 * 128 + 128)
    parts = [local_out[g, block * 32 : block * 32 + 32, lanes] for g in range(GROUPS)]
    local_a, local_b = joined(*parts, place % 2)
    zonal_a, zonal_b = [], []
    for spot in range(PLACES):
        lanes = slice(spot // 2 * 128, spot // 2 * 128 + 128)
        parts = [zonal_out[g, row * 8 : row * 8 + 8, lanes] for g in range(GROUPS)]
        first, second = joined(*parts, spot % 2)
        zonal_a.append(first)
        zonal_b.append(second)
    zonal_a, zonal_b = jnp.concatenate(zonal_a), jnp.concatenate(zonal_b)
    a = local_a + zonal_a.astype(bf16).astype(f32)
    b = local_b + zonal_b.astype(bf16).astype(f32)
    return a, b


def store_mixture(mixture, zonal_out, local_out):
    for row in range(ROWS):
        a, b = mixed_rows(row, zonal_out, local_out)
        mixture[row * WIDE : (row + 1) * WIDE, 0:128] = a
        mixture[row * WIDE : (row + 1) * WIDE, 128:256] = b


def store_packed(field, packed, edge_rows):
    low = low_lanes((WIDE, 128))
    for row in range(ROWS):
        packed[row] = field[row * WIDE : (row + 1) * WIDE, 0:128].astype(bf16)
    for row in range(16):
        first = field[row * WIDE : (row + 1) * WIDE, 128:256]
        second = field[(row + 16) * WIDE : (row + 17) * WIDE, 128:256]
        packed[ROWS + row] = jnp.where(low, first, swap_halves(second)).astype(bf16)
    for k in range(RIM):
        edge_rows[0, k] = field[k * WIDE : (k + 1) * WIDE, 0:CHANNELS].astype(bf16)
        row = ROWS - RIM + k
        edge_rows[1, k] = field[row * WIDE : (row + 1) * WIDE, 0:CHANNELS].astype(bf16)


def normalized(value, gain):
    average = jnp.mean(value, axis=-1, keepdims=True)
    centered = value - average
    variance = jnp.mean(centered * centered, axis=-1, keepdims=True)
    inverse = lax.rsqrt(variance + epsilon)
    unit = centered * inverse
    return unit, inverse, (unit * gain).astype(bf16)


def gelu_parts(value):
    square = value * value
    bent = jnp.tanh(gelu_scale * value * (1.0 + gelu_cube * square))
    share = 0.5 + 0.5 * bent
    return square, bent, share


def transposed_dot(left, right):
    return lax.dot_general(left, right, (((1,), (1,)), ((), ())), preferred_element_type=f32)


def backward(rows, mixture, adjoint, weight, gain, weight_in, weight_out, field, saved):
    normed_out, hidden_out, preact_out, update_out = saved
    unit, inverse, normed = normalized(mixture, gain)
    preact = jnp.dot(normed, weight_in[...], preferred_element_type=f32)
    square, bent, share = gelu_parts(preact)
    update = (weight * adjoint).astype(bf16)
    slope = share + 0.5 * preact * (1.0 - bent * bent) * gelu_scale * (
        1.0 + 3.0 * gelu_cube * square
    )
    grad_preact = (transposed_dot(update, weight_out[...]) * slope).astype(bf16)
    normed_out[rows] = normed
    hidden_out[rows] = (preact * share).astype(bf16)
    preact_out[rows] = grad_preact
    update_out[rows] = update
    grad = transposed_dot(grad_preact, weight_in[...]) * gain
    shared = jnp.mean(grad, axis=-1, keepdims=True)
    along = jnp.mean(grad * unit, axis=-1, keepdims=True)
    field[rows, 0:CHANNELS] = inverse * (grad - shared - unit * along)


CONV_IN = 8
CONV_SCRATCH = 9


def first_step(*refs):
    ins, refs = refs[:CONV_IN], refs[CONV_IN:]
    (weight_ref, state, gain, weight_in, weight_out, mixture_out, packed, edge_rows), refs = (
        refs[:8],
        refs[8:],
    )
    field, scratch = refs[0], refs[1:]
    mix(*ins, scratch)
    store_mixture(field, *scratch[-2:])

    @pl.loop(0, CELLS // CHUNK)
    def _(chunk):
        rows = pl.ds(pl.multiple_of(chunk * CHUNK, CHUNK), CHUNK)
        mixture = field[rows, 0:CHANNELS]
        mixture_out[rows] = mixture
        normed = normalized(mixture, gain[...])[2]
        preact = jnp.dot(normed, weight_in[...], preferred_element_type=f32)
        hidden = (preact * gelu_parts(preact)[2]).astype(bf16)
        update = jnp.dot(hidden, weight_out[...], preferred_element_type=f32)
        weight = weight_ref[rows].astype(f32)
        field[rows, 0:CHANNELS] = weight * (state[rows].astype(f32) + update)

    store_packed(field, packed, edge_rows)


def second_step(*refs):
    ins, refs = refs[:CONV_IN], refs[CONV_IN:]
    weight_ref, cotangent, gain, weight_in, weight_out, packed, edge_rows = refs[:7]
    saved, field, scratch = refs[7:11], refs[11], refs[12:]
    mix(*ins, scratch)
    store_mixture(field, *scratch[-2:])

    @pl.loop(0, CELLS // CHUNK)
    def _(chunk):
        rows = pl.ds(pl.multiple_of(chunk * CHUNK, CHUNK), CHUNK)
        backward(
            rows,
            field[rows, 0:CHANNELS],
            cotangent[rows].astype(f32),
            weight_ref[rows].astype(f32),
            gain[...],
            weight_in,
            weight_out,
            field,
            saved,
        )

    store_packed(field, packed, edge_rows)


def third_step(*refs):
    ins, refs = refs[:CONV_IN], refs[CONV_IN:]
    weight_ref, cotangent, mixture_in, gain, weight_in, weight_out = refs[:6]
    adjoint_out, packed, edge_rows = refs[6:9]
    saved, field, scratch = refs[9:13], refs[13], refs[14:]
    mix(*ins, scratch)
    store_mixture(field, *scratch[-2:])

    @pl.loop(0, CELLS // CHUNK)
    def _(chunk):
        rows = pl.ds(pl.multiple_of(chunk * CHUNK, CHUNK), CHUNK)
        weight = weight_ref[rows].astype(f32)
        adjoint = weight * cotangent[rows].astype(f32) + field[rows, 0:CHANNELS]
        adjoint_out[rows] = adjoint
        backward(
            rows, mixture_in[rows], adjoint, weight, gain[...], weight_in, weight_out, field, saved
        )

    store_packed(field, packed, edge_rows)


def last_step(*refs):
    ins, refs = refs[:CONV_IN - 1 + 1], refs[CONV_IN:]
    weight_ref, adjoint, out = refs[:3]
    scratch = refs[3:]
    mix(*ins, scratch)
    for row in range(ROWS):
        cells = slice(row * WIDE, (row + 1) * WIDE)
        a, b = mixed_rows(row, *scratch[-2:])
        weight, value = weight_ref[cells].astype(f32), adjoint[cells]
        kept = weight * value
        out[row, :, 0:128] = (kept[:, :128] + a)[:COLS]
        out[row, :, 128:CHANNELS] = (kept[:, 128:] + b[:, : CHANNELS - 128])[:COLS]


def packing(state, packed, edge_rows, field):
    for row in range(ROWS):
        field[row * WIDE : (row + 1) * WIDE, 0:CHANNELS] = state[
            row * WIDE : (row + 1) * WIDE
        ].astype(f32)
    store_packed(field, packed, edge_rows)


def conv_scratch():
    return [
        pltpu.VMEM((48, 112, 128), f32),
        pltpu.VMEM((GROUPS, ROWS, 104, 128), f32),
        pltpu.VMEM((2, 2 * RIM, 48, 128), f32),
        pltpu.VMEM((GROUPS, 20, 48, 128), f32),
        pltpu.VMEM((CHUNK, ZONAL_TILES * TILE), bf16),
        pltpu.VMEM((320, 7 * TILE), bf16),
        pltpu.VMEM((28 * TILE, TILE), bf16),
        pltpu.VMEM((GROUPS, CHUNK, TILE), f32),
        pltpu.VMEM((GROUPS, CHUNK, TILE), f32),
    ]


def shape(dims, dtype):
    return jax.ShapeDtypeStruct(dims, dtype)


def run(body, outs, args, name, conv=True, field=True):
    specs = [pl.BlockSpec(memory_space=pltpu.VMEM)] * len(args)
    if conv:
        specs[0] = pl.BlockSpec(memory_space=pltpu.SMEM)
    scratch = ([pltpu.VMEM((CELLS, 256), f32)] if field else []) + (conv_scratch() if conv else [])
    return pl.pallas_call(
        body,
        out_shape=outs,
        in_specs=specs,
        out_specs=[pl.BlockSpec(memory_space=pltpu.VMEM)] * len(outs),
        scratch_shapes=scratch,
        compiler_params=pltpu.CompilerParams(vmem_limit_bytes=52 * 2**20),
        name=name,
    )(*args)


PACKED = [shape((48, WIDE, 128), bf16), shape((2, RIM, WIDE, CHANNELS), bf16)]
SAVED = [
    shape((CELLS, CHANNELS), bf16),
    shape((CELLS, HIDDEN), bf16),
    shape((CELLS, HIDDEN), bf16),
    shape((CELLS, CHANNELS), bf16),
]


def flat_cells(block):
    padded = jnp.pad(block, ((0, 0), (0, WIDE - COLS), (0, 0)))
    return padded.reshape(CELLS, -1)


def column_dot(left, right):
    return lax.dot_general(left, right, (((0,), (0,)), ((), ())), preferred_element_type=f32)


def shards(
    ocean_state, ocean_mask, cotangent, kernel, zonal_taps, norm_gain, weight_in, weight_out
):
    at_top = lax.axis_index("band") == lax.axis_size("band") - 1
    parity = (lax.axis_index("blk") % 2).astype(jnp.int32).reshape(1)
    state = flat_cells(ocean_state)
    packed, edge_rows = run(packing, PACKED, (state,), "packing", conv=False)
    halo = halos(packed, edge_rows)
    weight = flat_cells(jnp.broadcast_to(ocean_mask[:, :, None].astype(bf16), ocean_state.shape))
    cells = flat_cells(cotangent)
    gain = norm_gain[None]
    zonal_v, zonal_back = zonal_entries(zonal_taps), zonal_entries(zonal_taps[::-1])
    local_v, local_back = local_entries(kernel), local_entries(kernel[::-1, ::-1])
    north_v = local_v[:, 56:]
    north_back = jnp.where(at_top, north_v, local_back[:, 56:])
    forth = (zonal_v, local_v, north_v)
    back = (zonal_back, local_back, north_back)
    mlp = (gain, weight_in, weight_out)
    mixture, packed, edge_rows = run(
        first_step,
        [shape((CELLS, CHANNELS), f32)] + PACKED,
        (parity, packed, *halo, *forth, weight, state, *mlp),
        "first_step",
    )
    halo = halos(packed, edge_rows)
    packed, edge_rows, *saved_second = run(
        second_step,
        PACKED + SAVED,
        (parity, packed, *halo, *forth, weight, cells, *mlp),
        "second_step",
    )
    halo = halos(packed, edge_rows)
    adjoint, packed, edge_rows, *saved_first = run(
        third_step,
        [shape((CELLS, CHANNELS), f32)] + PACKED + SAVED,
        (parity, packed, *halo, *back, weight, cells, mixture, *mlp),
        "third_step",
    )
    total_in = jnp.zeros((CHANNELS, HIDDEN), f32)
    total_out = jnp.zeros((CHANNELS, HIDDEN), f32)
    for normed, hidden, grad_preact, update in (saved_second, saved_first):
        total_in = total_in + column_dot(normed, grad_preact)
        total_out = total_out + column_dot(update, hidden)
    halo = halos(packed, edge_rows)
    (grad_state,) = run(
        last_step,
        [shape((ROWS, COLS, CHANNELS), f32)],
        (parity, packed, *halo, *back, weight, adjoint),
        "last_step",
        field=False,
    )
    terms = jnp.concatenate([total_in, total_out]).reshape(2 * CHANNELS, -1, 128)
    terms = summed(terms.swapaxes(0, 1).reshape(-1, 128)).astype(f32)
    terms = terms.reshape(-1, 2 * CHANNELS, 128).swapaxes(0, 1).reshape(2 * CHANNELS, -1)
    cell_count = ROWS * lax.axis_size("band") * COLS * lax.axis_size("blk")
    scaling = 1.0 / math.sqrt(cell_count)
    return (grad_state, terms[:CHANNELS] * scaling, terms[CHANNELS:].T * scaling)


def solution(mesh):
    return jax.shard_map(
        shards,
        mesh=mesh,
        in_specs=(
            P("band", "blk", None),
            P("band", "blk"),
            P("band", "blk", None),
            P(),
            P(),
            P(),
            P(),
            P(),
        ),
        out_specs=(P("band", "blk", None), P(), P()),
        check_vma=False,
    )
```

```python
import math

import jax
import jax.numpy as jnp
from jax import lax
from jax.experimental import pallas as pl
from jax.experimental.pallas import tpu as pltpu
from jax.sharding import PartitionSpec as P

ROWS, COLS, CHANNELS, HIDDEN = 32, 30, 192, 768
WIDE = 32
CELLS = ROWS * WIDE
RIM, HALF, GROUP, GROUPS, PLACES = 3, 30, 64, 3, 4
ZONAL_TILES, LOCAL_TILES = 24, 21
TILE = GROUP * PLACES
CHUNK = 256
VMEM_LIMIT = 24 * 2**20
bf16, f32 = jnp.bfloat16, jnp.float32
epsilon = 1e-06
gelu_scale, gelu_cube = math.sqrt(2.0 / math.pi), 0.044715


def ways(axis, low, count):
    position = (lax.axis_index(axis) // low) % count
    pairs = [
        [(i, i ^ (low * step)) for i in range(lax.axis_size(axis))] for step in range(count)
    ]
    return position, pairs


def scattered_sum(parts, axis, low, count):
    position, pairs = ways(axis, low, count)
    parts = parts.reshape((count, -1) + parts.shape[1:])
    total = lax.dynamic_index_in_dim(parts, position, 0, False)
    arrived = []
    for step in range(1, count):
        piece = lax.dynamic_index_in_dim(parts, position ^ step, 0, False).astype(bf16)
        arrived.append(lax.ppermute(piece, axis, pairs[step]))
    for piece in arrived:
        total = total + piece.astype(f32)
    return total


def gathered(value, axis, low, count):
    position, pairs = ways(axis, low, count)
    whole = jnp.zeros((count,) + value.shape, value.dtype)
    whole = lax.dynamic_update_index_in_dim(whole, value, position, 0)
    for step in range(1, count):
        piece = lax.ppermute(value, axis, pairs[step])
        whole = lax.dynamic_update_index_in_dim(whole, piece, position ^ step, 0)
    return whole


def doubled(value, axis, step):
    sent = value.astype(bf16)
    pairs = [(i, i ^ step) for i in range(lax.axis_size(axis))]
    return sent.astype(f32) + lax.ppermute(sent, axis, pairs).astype(f32)


def summed(value):
    value = scattered_sum(value, "blk", 1, 2)[0]
    value = scattered_sum(value, "blk", 2, 4)
    for axis, step in (("blk", 8), ("blk", 24), ("band", 1), ("band", 2), ("band", 6)):
        value = doubled(value, axis, step)
    value = gathered(value.astype(bf16), "blk", 2, 4).reshape(-1, 128)
    return gathered(value, "blk", 1, 2)


def block_swaps(packed):
    blocks = lax.axis_size("blk")
    inner = [(i, i ^ 1) for i in range(blocks)]
    outer = [(i, (i + 1) % blocks if i % 2 else (i - 1) % blocks) for i in range(blocks)]
    return lax.ppermute(packed, "blk", inner), lax.ppermute(packed, "blk", outer)


def rim_swaps(to_near, to_far, turned):
    bands, blocks = lax.axis_size("band"), lax.axis_size("blk")
    near = [
        (b * blocks + i, (b ^ 1) * blocks + i) for b in range(bands) for i in range(blocks)
    ]
    far = [
        (b * blocks + i, (b + 1 if b % 2 else b - 1) * blocks + i)
        for b in range(1, bands - 1)
        for i in range(blocks)
    ]
    last = (bands - 1) * blocks
    far += [(last + i, last + blocks - 1 - i) for i in range(blocks)]
    far += [(i, i ^ 1) for i in range(blocks)]
    span = COLS + 2 * RIM
    turned = jnp.concatenate([turned[:, :span][:, ::-1], turned[:, span:]], axis=1)
    to_far = jnp.where(lax.axis_index("band") == bands - 1, turned, to_far)
    return (
        lax.ppermute(to_near, ("band", "blk"), near),
        lax.ppermute(to_far, ("band", "blk"), far),
    )


def zonal_rows(taps, odd_block):
    padded = jnp.pad(taps.astype(f32), ((24, 27), (0, 0))).reshape(-1, GROUPS, GROUP)
    padded = jnp.swapaxes(padded, 0, 1)
    padded = jnp.concatenate([padded, padded], axis=2)
    near = jnp.where(odd_block, padded[:, 0:88], padded[:, 23:111])
    far = jnp.where(odd_block, padded[:, 53:109], padded[:, 0:56])
    return near, far


def local_rows(kernel):
    padded = jnp.pad(kernel.astype(f32), ((4, 4), (0, 1), (0, 0)))
    padded = padded.reshape(15, 8, GROUPS, GROUP).transpose(2, 0, 1, 3)
    return jnp.concatenate([padded, padded], axis=3)


def low_lanes(shape):
    return lax.broadcasted_iota(jnp.int32, shape, len(shape) - 1) < GROUP


def swap_halves(value):
    return pltpu.roll(value, GROUP, value.ndim - 1)


def units():
    same = (
        lax.broadcasted_iota(jnp.int32, (GROUP, 128), 0)
        == lax.broadcasted_iota(jnp.int32, (GROUP, 128), 1) % GROUP
    )
    return jnp.where(same, 1.0, 0.0).astype(bf16)


def fill(out, unit, start, count, picks):
    low = low_lanes((8, 128))
    for half in range(2):
        rows = jnp.where(low, picks[2 * half], picks[2 * half + 1])
        for k in range(count):
            row = jnp.broadcast_to(rows[k : k + 1], (16, 128)).astype(bf16)
            block = jnp.concatenate([row] * (GROUP // 16)) * unit
            place = start + k * TILE
            out[place : place + GROUP, half * 128 : half * 128 + 128] = block


def zonal_matrix(out, unit, g, rows, count):
    for i in range(PLACES):
        for m in range(count // 8):
            base = [32 * m + 8 * (i - o) + 24 for o in range(PLACES)]
            fill(out, unit, m * 8 * TILE + i * GROUP, 8, [rows[g, k : k + 8] for k in base])


def local_matrix(out, unit, g, rows, blocks, start=0):
    for b in blocks:
        for i in range(PLACES):
            base = [4 * (b - 1) + i - o + RIM + 4 for o in range(PLACES)]
            fill(out, unit, start + i * GROUP, 7, [rows[g, k] for k in base])
        start += 7 * TILE


def pair_columns(wide, pairs, length):
    low = low_lanes((length, 128))
    for r in range(ROWS):
        value = wide[r, 0 : length + 8]
        turned = swap_halves(value)
        pairs[0, r] = jnp.where(low, value[:length], turned[8:])
        pairs[1, r] = jnp.where(low, turned[:length], value[8:])
    for r in range(16):
        value = wide[32 + r, 0 : length + 8]
        turned = swap_halves(value)
        pairs[2, r] = jnp.where(low, value[:length], turned[8:])
        pairs[2, 16 + r] = jnp.where(low, turned[:length], value[8:])


def zonal_product(g, pairs, left, rows, matrix, count):
    zonal_matrix(matrix, units(), g, rows, count)
    for tile in range(count):
        start = tile % 8 + 32 * (tile // 8)
        for half in range(2):
            value = pairs[g, :, start + 16 * half : start + 16 * half + 8, :]
            column = tile * TILE + half * 128
            left[:, column : column + 128] = value.reshape(CHUNK, 128).astype(bf16)
    return jnp.dot(left[...], matrix[0 : count * TILE], preferred_element_type=f32)


def near_body(block_odd, own, inner, rows, out, wide, pairs, left, matrix):
    odd = block_odd[0] == 1
    for r in range(48):
        wide[r, 0:8] = jnp.zeros((8, 128), f32)
        wide[r, 56:72] = jnp.zeros((16, 128), f32)

    @pl.when(odd)
    def _():
        for r in range(48):
            wide[r, 0:32] = inner[r].astype(f32)
            wide[r, 30:62] = own[r].astype(f32)

    @pl.when(jnp.logical_not(odd))
    def _():
        for r in range(48):
            wide[r, 7:39] = own[r].astype(f32)
            wide[r, 37:69] = inner[r].astype(f32)

    pair_columns(wide, pairs, 64)

    @pl.loop(0, GROUPS)
    def _(g):
        out[g] = zonal_product(g, pairs, left, rows, matrix, 16)


def rims_body(block_odd, band_odd, own, inner, outer, near_out, far_out, turned_out, rim):
    odd, upper = block_odd[0] == 1, band_odd[0] == 1
    places = list(range(3)) + list(range(32, 35)) + list(range(29, 32)) + list(range(45, 48))
    for k, r in enumerate(places):
        ins, outs = inner[r].astype(f32), outer[r].astype(f32)
        west, east = jnp.where(odd, ins, outs), jnp.where(odd, outs, ins)
        rim[k, 3:35] = own[r].astype(f32)
        rim[k, 0:3] = west[27:30]
        rim[k, 33:36] = east[0:3]
        rim[k, 36:40] = jnp.zeros((4, 128), f32)
    for k in range(6):
        low, high = rim[k], rim[6 + k]
        near_out[k] = jnp.where(upper, low, high).astype(bf16)
        far_out[k] = jnp.where(upper, high, low).astype(bf16)
        value = rim[8 - k] if k < 3 else swap_halves(rim[14 - k])
        turned_out[k] = value.astype(bf16)


def inner_body(
    block_odd, own, inner, outer, zonal, far, local, zonal_out, local_out,
    wide, pairs, field, row_pairs, zonal_left, local_left, matrix,
):
    odd = block_odd[0] == 1
    for r in range(48):
        wide[r] = jnp.zeros((48, 128), f32)

    @pl.when(odd)
    def _():
        for r in range(48):
            wide[r, 7:39] = outer[r].astype(f32)

    @pl.when(jnp.logical_not(odd))
    def _():
        for r in range(48):
            wide[r, 0:32] = outer[r].astype(f32)

    pair_columns(wide, pairs, 40)
    for r in range(48):
        ins, outs = inner[r].astype(f32), outer[r].astype(f32)
        west, east = jnp.where(odd, ins, outs), jnp.where(odd, outs, ins)
        field[r, 8:40] = own[r].astype(f32)
        field[r, 5:8] = west[27:30]
        field[r, 38:46] = east[0:8]
    low = low_lanes((48, 128))
    for q in range(16):
        first, second = field[2 * q], field[2 * q + 1]
        row_pairs[0, q] = jnp.where(low, first, swap_halves(second))
        row_pairs[1, q] = jnp.where(low, swap_halves(first), second)
        first, second = field[32 + 2 * q % 16], field[33 + 2 * q % 16]
        if q < 8:
            row_pairs[2, q] = jnp.where(low, first, swap_halves(second))
        else:
            row_pairs[2, q] = jnp.where(low, swap_halves(first), second)
    depth = 7 * TILE

    @pl.loop(0, GROUPS)
    def _(g):
        zonal_out[g] = zonal[g] + zonal_product(g, pairs, zonal_left, far, matrix, 8)
        local_matrix(matrix, units(), g, local, range(3))
        for shift in range(7):
            for half in range(2):
                column = shift * TILE + half * 128
                for block in range(8):
                    value = row_pairs[g, 2 * block + half, 5 + shift : 37 + shift, :]
                    local_left[block * 32 : block * 32 + 32, column : column + 128] = (
                        value.astype(bf16)
                    )
        local_out[g] = jnp.dot(
            local_left[...], matrix[depth : 2 * depth], preferred_element_type=f32
        )
        local_out[g, 32:256] += jnp.dot(
            local_left[0:224], matrix[0:depth], preferred_element_type=f32
        )
        local_out[g, 0:224] += jnp.dot(
            local_left[32:256], matrix[2 * depth : 3 * depth], preferred_element_type=f32
        )


def edges(band_odd, near_rows, far_rows, local, north, edge, rim, row_pairs, left, matrix):
    upper, bottom = band_odd[0] == 1, band_odd[1] == 1
    low = low_lanes((48, 128))
    nothing = jnp.zeros((48, 128), f32)
    for k in range(6):
        near, far = near_rows[k].astype(f32), far_rows[k].astype(f32)
        rim[k, 5:45] = jnp.where(upper, near, jnp.where(bottom, jnp.zeros_like(far), far))
        rim[6 + k, 5:45] = jnp.where(upper, far, near)
    below = [(nothing, nothing)] + [(rim[k], rim[3 + k]) for k in range(3)]
    above = [(rim[6 + k], rim[9 + k]) for k in range(3)] + [(nothing, nothing)]
    for side, rows in enumerate((below, above)):
        for half in range(2):
            (a, c), (b, d) = rows[2 * half], rows[2 * half + 1]
            place = 2 * side + half
            row_pairs[0, place] = jnp.where(low, a, swap_halves(b))
            row_pairs[1, place] = jnp.where(low, swap_halves(a), b)
            if side == 0:
                row_pairs[2, place] = jnp.where(low, swap_halves(c), d)
            else:
                row_pairs[2, place] = jnp.where(low, c, swap_halves(d))

    @pl.loop(0, GROUPS)
    def _(g):
        for side in range(2):
            for shift in range(7):
                for half in range(2):
                    column = shift * TILE + half * 128
                    value = row_pairs[g, 2 * side + half, 5 + shift : 37 + shift, :]
                    left[side * 32 : side * 32 + 32, column : column + 128] = value.astype(bf16)
        unit, depth = units(), 7 * TILE
        local_matrix(matrix, unit, g, local, (0,))
        local_matrix(matrix, unit, g, north, (2,), depth)
        edge[g, 0:32] = jnp.dot(left[0:32], matrix[0:depth], preferred_element_type=f32)
        edge[g, 32:64] = jnp.dot(
            left[32:64], matrix[depth : 2 * depth], preferred_element_type=f32
        )


def mixed_rows(row, zonal_out, local_out, edge):
    block, place = row // PLACES, row % PLACES

    def joined(first, second, third, odd):
        mask = low_lanes(first.shape)
        if odd:
            return jnp.where(mask, swap_halves(first), second), swap_halves(third)
        return jnp.where(mask, first, swap_halves(second)), third

    lanes = slice(place // 2 * 128, place // 2 * 128 + 128)
    parts = [local_out[g, block * 32 : block * 32 + 32, lanes] for g in range(GROUPS)]
    if block == 0:
        parts = [parts[g] + edge[g, 0:32, lanes] for g in range(GROUPS)]
    if block == ROWS // PLACES - 1:
        parts = [parts[g] + edge[g, 32:64, lanes] for g in range(GROUPS)]
    local_a, local_b = joined(*parts, place % 2)
    zonal_a, zonal_b = [], []
    for spot in range(PLACES):
        lanes = slice(spot // 2 * 128, spot // 2 * 128 + 128)
        parts = [zonal_out[g, row * 8 : row * 8 + 8, lanes] for g in range(GROUPS)]
        first, second = joined(*parts, spot % 2)
        zonal_a.append(first)
        zonal_b.append(second)
    zonal_a, zonal_b = jnp.concatenate(zonal_a), jnp.concatenate(zonal_b)
    a = local_a + zonal_a.astype(bf16).astype(f32)
    b = local_b + zonal_b.astype(bf16).astype(f32)
    return a, b


def store_mixture(mixture, *parts):
    for row in range(ROWS):
        a, b = mixed_rows(row, *parts)
        mixture[row * WIDE : (row + 1) * WIDE, 0:128] = a
        mixture[row * WIDE : (row + 1) * WIDE, 128:256] = b


def store_packed(field, packed):
    low = low_lanes((WIDE, 128))
    for row in range(ROWS):
        packed[row] = field[row * WIDE : (row + 1) * WIDE, 0:128].astype(bf16)
    for row in range(16):
        first = field[row * WIDE : (row + 1) * WIDE, 128:256]
        second = field[(row + 16) * WIDE : (row + 17) * WIDE, 128:256]
        packed[ROWS + row] = jnp.where(low, first, swap_halves(second)).astype(bf16)


def normalized(value, gain):
    average = jnp.mean(value, axis=-1, keepdims=True)
    centered = value - average
    variance = jnp.mean(centered * centered, axis=-1, keepdims=True)
    inverse = lax.rsqrt(variance + epsilon)
    unit = centered * inverse
    return unit, inverse, (unit * gain).astype(bf16)


def gelu_parts(value):
    square = value * value
    bent = jnp.tanh(gelu_scale * value * (1.0 + gelu_cube * square))
    share = 0.5 + 0.5 * bent
    return square, bent, share


def transposed_dot(left, right):
    return lax.dot_general(left, right, (((1,), (1,)), ((), ())), preferred_element_type=f32)


def backward(rows, mixture, adjoint, weight, gain, weight_in, weight_out, field, saved):
    normed_out, hidden_out, preact_out, update_out = saved
    unit, inverse, normed = normalized(mixture, gain)
    preact = jnp.dot(normed, weight_in[...], preferred_element_type=f32)
    square, bent, share = gelu_parts(preact)
    update = (weight * adjoint).astype(bf16)
    slope = share + 0.5 * preact * (1.0 - bent * bent) * gelu_scale * (
        1.0 + 3.0 * gelu_cube * square
    )
    grad_preact = (transposed_dot(update, weight_out[...]) * slope).astype(bf16)
    normed_out[rows] = normed
    hidden_out[rows] = (preact * share).astype(bf16)
    preact_out[rows] = grad_preact
    update_out[rows] = update
    grad = transposed_dot(grad_preact, weight_in[...]) * gain
    shared = jnp.mean(grad, axis=-1, keepdims=True)
    along = jnp.mean(grad * unit, axis=-1, keepdims=True)
    field[rows, 0:CHANNELS] = inverse * (grad - shared - unit * along)


PARTS_IN = 7
PARTS_SCRATCH = 4


def joined_parts(ins, scratch):
    band_odd, near_rows, far_rows, zonal, inner, local, north = ins
    edges(band_odd, near_rows, far_rows, local, north, *scratch)
    return zonal, inner, scratch[0]


def first_step(*refs):
    ins, refs = refs[:PARTS_IN], refs[PARTS_IN:]
    (weight_ref, state, gain, weight_in, weight_out, mixture_out, packed), refs = (
        refs[:7],
        refs[7:],
    )
    field, scratch = refs[0], refs[1:]
    store_mixture(field, *joined_parts(ins, scratch))

    @pl.loop(0, CELLS // CHUNK)
    def _(chunk):
        rows = pl.ds(pl.multiple_of(chunk * CHUNK, CHUNK), CHUNK)
        mixture = field[rows, 0:CHANNELS]
        mixture_out[rows] = mixture
        normed = normalized(mixture, gain[...])[2]
        preact = jnp.dot(normed, weight_in[...], preferred_element_type=f32)
        hidden = (preact * gelu_parts(preact)[2]).astype(bf16)
        update = jnp.dot(hidden, weight_out[...], preferred_element_type=f32)
        weight = weight_ref[rows].astype(f32)
        field[rows, 0:CHANNELS] = weight * (state[rows].astype(f32) + update)

    store_packed(field, packed)


def second_step(*refs):
    ins, refs = refs[:PARTS_IN], refs[PARTS_IN:]
    weight_ref, cotangent, gain, weight_in, weight_out, packed, totals = refs[:7]
    field, saved, scratch = refs[7], refs[8:12], refs[12:]
    store_mixture(field, *joined_parts(ins, scratch))

    @pl.loop(0, CELLS // CHUNK)
    def _(chunk):
        rows = pl.ds(pl.multiple_of(chunk * CHUNK, CHUNK), CHUNK)
        backward(
            rows,
            field[rows, 0:CHANNELS],
            cotangent[rows].astype(f32),
            weight_ref[rows].astype(f32),
            gain[...],
            weight_in,
            weight_out,
            field,
            saved,
        )

    store_totals(*saved, totals)
    store_packed(field, packed)


def third_step(*refs):
    ins, refs = refs[:PARTS_IN], refs[PARTS_IN:]
    weight_ref, cotangent, mixture_in, before, gain, weight_in, weight_out = refs[:7]
    adjoint_out, packed, totals = refs[7:10]
    field, saved, scratch = refs[10], refs[11:15], refs[15:]
    store_mixture(field, *joined_parts(ins, scratch))

    @pl.loop(0, CELLS // CHUNK)
    def _(chunk):
        rows = pl.ds(pl.multiple_of(chunk * CHUNK, CHUNK), CHUNK)
        weight = weight_ref[rows].astype(f32)
        adjoint = weight * cotangent[rows].astype(f32) + field[rows, 0:CHANNELS]
        adjoint_out[rows] = adjoint
        backward(
            rows, mixture_in[rows], adjoint, weight, gain[...], weight_in, weight_out, field, saved
        )

    store_totals(*saved, totals, before)
    store_packed(field, packed)


def last_step(*refs):
    ins, refs = refs[:PARTS_IN], refs[PARTS_IN:]
    weight_ref, adjoint, out = refs[:3]
    parts = joined_parts(ins, refs[3:])
    for row in range(ROWS):
        cells = slice(row * WIDE, (row + 1) * WIDE)
        a, b = mixed_rows(row, *parts)
        weight, value = weight_ref[cells].astype(f32), adjoint[cells]
        kept = weight * value
        out[row, :, 0:128] = (kept[:, :128] + a)[:COLS]
        out[row, :, 128:CHANNELS] = (kept[:, 128:] + b[:, : CHANNELS - 128])[:COLS]


def column_dot(left, right):
    return lax.dot_general(left, right, (((0,), (0,)), ((), ())), preferred_element_type=f32)


def store_totals(normed, hidden, grad_preact, update, out, before=None):
    for index, (left, right) in enumerate(((normed, grad_preact), (update, hidden))):
        product = column_dot(left[...], right[...])
        for k in range(HIDDEN // 128):
            rows = slice(k * CHANNELS, (k + 1) * CHANNELS)
            part = product[:, k * 128 : (k + 1) * 128]
            out[index, rows] = part if before is None else before[index, rows] + part


def packing(state, packed, field):
    for row in range(ROWS):
        field[row * WIDE : (row + 1) * WIDE, 0:CHANNELS] = state[
            row * WIDE : (row + 1) * WIDE
        ].astype(f32)
    store_packed(field, packed)


PARTS = [
    pltpu.VMEM((GROUPS, 64, TILE), f32),
    pltpu.VMEM((12, 48, 128), f32),
    pltpu.VMEM((GROUPS, 4, 48, 128), f32),
    pltpu.VMEM((64, 7 * TILE), bf16),
    pltpu.VMEM((14 * TILE, TILE), bf16),
]
FIELD = [pltpu.VMEM((CELLS, 256), f32)]


def shape(dims, dtype):
    return jax.ShapeDtypeStruct(dims, dtype)


def run(body, outs, scalars, args, scratch, name, us=1.0, after=()):
    vmem = pl.BlockSpec(memory_space=pltpu.VMEM)
    count = len(scalars) + len(args)

    def called(*refs):
        body(*refs[:count], *refs[count + len(after) :])

    return pl.pallas_call(
        called,
        out_shape=outs,
        in_specs=[pl.BlockSpec(memory_space=pltpu.SMEM)] * len(scalars)
        + [vmem] * len(args)
        + [pl.BlockSpec(memory_space=pl.ANY)] * len(after),
        out_specs=[vmem] * len(outs),
        scratch_shapes=scratch,
        compiler_params=pltpu.CompilerParams(vmem_limit_bytes=VMEM_LIMIT),
        cost_estimate=pl.CostEstimate(
            flops=int(us * 1.1e9), bytes_accessed=int(us * 1e6), transcendentals=0
        ),
        name=name,
    )(*scalars, *args, *after)


PACKED = [shape((48, WIDE, 128), bf16)]
SAVED = [
    pltpu.VMEM((CELLS, CHANNELS), bf16),
    pltpu.VMEM((CELLS, HIDDEN), bf16),
    pltpu.VMEM((CELLS, HIDDEN), bf16),
    pltpu.VMEM((CELLS, CHANNELS), bf16),
]


def flat_cells(block):
    padded = jnp.pad(block, ((0, 0), (0, WIDE - COLS), (0, 0)))
    return padded.reshape(CELLS, -1)


TOTALS = shape((2, HIDDEN // 128 * CHANNELS, 128), f32)
ZONAL = shape((GROUPS, CHUNK, TILE), f32)
RIMS = shape((6, 40, 128), bf16)
def filtered(packed, odds, rows, ready=()):
    block_odd, band_odd = odds
    near, far, local, north = rows
    inner, outer = block_swaps(packed)
    (zonal,) = run(
        near_body,
        [ZONAL],
        (block_odd,),
        (packed, inner, near),
        [
            pltpu.VMEM((48, 72, 128), f32),
            pltpu.VMEM((GROUPS, ROWS, 64, 128), f32),
            pltpu.VMEM((CHUNK, 16 * TILE), bf16),
            pltpu.VMEM((16 * TILE, TILE), bf16),
        ],
        "near_zonal",
        4.0,
        after=ready,
    )
    rims = run(
        rims_body,
        [RIMS] * 3,
        odds,
        (packed, inner, outer),
        [pltpu.VMEM((12, 40, 128), f32)],
        "rims",
        0.3,
        after=(zonal,),
    )
    near_rows, far_rows = rim_swaps(*rims)
    zonal, mixed = run(
        inner_body,
        [ZONAL, ZONAL],
        (block_odd,),
        (packed, inner, outer, zonal, far, local),
        [
            pltpu.VMEM((48, 48, 128), f32),
            pltpu.VMEM((GROUPS, ROWS, 40, 128), f32),
            pltpu.VMEM((48, 48, 128), f32),
            pltpu.VMEM((GROUPS, 16, 48, 128), f32),
            pltpu.VMEM((CHUNK, 8 * TILE), bf16),
            pltpu.VMEM((CHUNK, 7 * TILE), bf16),
            pltpu.VMEM((LOCAL_TILES * TILE, TILE), bf16),
        ],
        "inner_filters",
        6.0,
    )
    return near_rows, far_rows, zonal, mixed, local, north


def shards(
    ocean_state, ocean_mask, cotangent, kernel, zonal_taps, norm_gain, weight_in, weight_out
):
    band = lax.axis_index("band")
    at_top = band == lax.axis_size("band") - 1
    block_odd = lax.axis_index("blk") % 2
    odds = (
        block_odd.astype(jnp.int32).reshape(1),
        jnp.stack([band % 2, (band == 0).astype(jnp.int32)]),
    )
    state = flat_cells(ocean_state)
    (packed,) = run(packing, PACKED, (), (state,), FIELD, "packing")
    weight = flat_cells(jnp.broadcast_to(ocean_mask[:, :, None].astype(bf16), ocean_state.shape))
    cells = flat_cells(cotangent)
    mlp = (norm_gain[None], weight_in, weight_out)
    zonal_forth = zonal_rows(zonal_taps, block_odd == 1)
    zonal_back = zonal_rows(zonal_taps[::-1], block_odd == 1)
    local_forth, local_back = local_rows(kernel), local_rows(kernel[::-1, ::-1])
    north_back = jnp.where(at_top, local_forth, local_back)
    forth = (*zonal_forth, local_forth, local_forth)
    back = (*zonal_back, local_back, north_back)
    ready = (cells, weight, weight_out, *back)
    parts = filtered(packed, odds, forth, ready)
    mixture, packed = run(
        first_step,
        [shape((CELLS, CHANNELS), f32)] + PACKED,
        odds[1:],
        (*parts, weight, state, *mlp),
        FIELD + PARTS,
        "first_step",
        5.0,
    )
    parts = filtered(packed, odds, forth)
    packed, totals = run(
        second_step,
        PACKED + [TOTALS],
        odds[1:],
        (*parts, weight, cells, *mlp),
        FIELD + SAVED + PARTS,
        "second_step",
        7.0,
    )
    parts = filtered(packed, odds, back)
    adjoint, packed, totals = run(
        third_step,
        [shape((CELLS, CHANNELS), f32)] + PACKED + [TOTALS],
        odds[1:],
        (*parts, weight, cells, mixture, totals, *mlp),
        FIELD + SAVED + PARTS,
        "third_step",
        7.0,
    )
    parts = filtered(packed, odds, back)
    (grad_state,) = run(
        last_step,
        [shape((ROWS, COLS, CHANNELS), f32)],
        odds[1:],
        (*parts, weight, adjoint),
        PARTS,
        "last_step",
        3.0,
    )
    sums = summed(totals)
    cell_count = ROWS * lax.axis_size("band") * COLS * lax.axis_size("blk")
    scaling = 1.0 / math.sqrt(cell_count)
    whole = shape((CHANNELS, HIDDEN), f32)

    def scaled(sums_ref, in_out, out_out):
        for k in range(HIDDEN // 128):
            for out, index in ((in_out, 0), (out_out, 1)):
                value = sums_ref[index, k * CHANNELS : (k + 1) * CHANNELS].astype(f32)
                out[:, k * 128 : (k + 1) * 128] = value * scaling

    grad_in, grad_out = run(scaled, [whole, whole], (), (sums,), [], "scaled", 0.5)
    return (grad_state, grad_in, grad_out.T)


def solution(mesh):
    return jax.shard_map(
        shards,
        mesh=mesh,
        in_specs=(
            P("band", "blk", None),
            P("band", "blk"),
            P("band", "blk", None),
            P(),
            P(),
            P(),
            P(),
            P(),
        ),
        out_specs=(P("band", "blk", None), P(), P()),
        check_vma=False,
    )
```

```python
import math

import jax
import jax.numpy as jnp
from jax import lax
from jax.experimental import pallas as pl
from jax.experimental.pallas import tpu as pltpu
from jax.sharding import PartitionSpec as P

ROWS, COLS, CHANNELS, HIDDEN = 32, 30, 192, 768
WIDE = 32
CELLS = ROWS * WIDE
RIM, HALF, GROUP, GROUPS, PLACES = 3, 30, 64, 3, 4
ZONAL_TILES, LOCAL_TILES = 24, 21
TILE = GROUP * PLACES
CHUNK = 256
VMEM_LIMIT = 24 * 2**20
bf16, f32 = jnp.bfloat16, jnp.float32
epsilon = 1e-06
gelu_scale, gelu_cube = math.sqrt(2.0 / math.pi), 0.044715


def ways(axis, low, count):
    position = (lax.axis_index(axis) // low) % count
    pairs = [
        [(i, i ^ (low * step)) for i in range(lax.axis_size(axis))] for step in range(count)
    ]
    return position, pairs


def scattered_sum(parts, axis, low, count):
    position, pairs = ways(axis, low, count)
    parts = parts.reshape((count, -1) + parts.shape[1:])
    total = lax.dynamic_index_in_dim(parts, position, 0, False)
    arrived = []
    for step in range(1, count):
        piece = lax.dynamic_index_in_dim(parts, position ^ step, 0, False).astype(bf16)
        arrived.append(lax.ppermute(piece, axis, pairs[step]))
    for piece in arrived:
        total = total + piece.astype(f32)
    return total


def gathered(value, axis, low, count):
    position, pairs = ways(axis, low, count)
    whole = jnp.zeros((count,) + value.shape, value.dtype)
    whole = lax.dynamic_update_index_in_dim(whole, value, position, 0)
    for step in range(1, count):
        piece = lax.ppermute(value, axis, pairs[step])
        whole = lax.dynamic_update_index_in_dim(whole, piece, position ^ step, 0)
    return whole


def doubled(value, axis, step):
    sent = value.astype(bf16)
    pairs = [(i, i ^ step) for i in range(lax.axis_size(axis))]
    return sent.astype(f32) + lax.ppermute(sent, axis, pairs).astype(f32)


def summed(value):
    value = scattered_sum(value, "blk", 1, 2)[0]
    value = scattered_sum(value, "blk", 2, 4)
    for axis, step in (("blk", 8), ("blk", 24), ("band", 1), ("band", 2), ("band", 6)):
        value = doubled(value, axis, step)
    value = gathered(value.astype(bf16), "blk", 2, 4).reshape(-1, 128)
    return gathered(value, "blk", 1, 2)


def block_swaps(packed):
    blocks = lax.axis_size("blk")
    inner = [(i, i ^ 1) for i in range(blocks)]
    outer = [(i, (i + 1) % blocks if i % 2 else (i - 1) % blocks) for i in range(blocks)]
    return lax.ppermute(packed, "blk", inner), lax.ppermute(packed, "blk", outer)


def rim_swaps(to_near, to_far):
    bands, blocks = lax.axis_size("band"), lax.axis_size("blk")
    near = [
        (b * blocks + i, (b ^ 1) * blocks + i) for b in range(bands) for i in range(blocks)
    ]
    far = [
        (b * blocks + i, (b + 1 if b % 2 else b - 1) * blocks + i)
        for b in range(1, bands - 1)
        for i in range(blocks)
    ]
    last = (bands - 1) * blocks
    far += [(last + i, last + blocks - 1 - i) for i in range(blocks)]
    far += [(i, i ^ 1) for i in range(blocks)]
    return (
        lax.ppermute(to_near, ("band", "blk"), near),
        lax.ppermute(to_far, ("band", "blk"), far),
    )


def zonal_rows(taps, odd_block):
    padded = jnp.pad(taps.astype(f32), ((24, 27), (0, 0))).reshape(-1, GROUPS, GROUP)
    padded = jnp.swapaxes(padded, 0, 1)
    padded = jnp.concatenate([padded, padded], axis=2)
    near = jnp.where(odd_block, padded[:, 0:88], padded[:, 23:111])
    far = jnp.where(odd_block, padded[:, 53:109], padded[:, 0:56])
    return near, far


def local_rows(kernel):
    padded = jnp.pad(kernel.astype(f32), ((4, 4), (0, 1), (0, 0)))
    padded = padded.reshape(15, 8, GROUPS, GROUP).transpose(2, 0, 1, 3)
    return jnp.concatenate([padded, padded], axis=3)


def low_lanes(shape):
    return lax.broadcasted_iota(jnp.int32, shape, len(shape) - 1) < GROUP


def swap_halves(value):
    return pltpu.roll(value, GROUP, value.ndim - 1)


def units():
    same = (
        lax.broadcasted_iota(jnp.int32, (GROUP, 128), 0)
        == lax.broadcasted_iota(jnp.int32, (GROUP, 128), 1) % GROUP
    )
    return jnp.where(same, 1.0, 0.0).astype(bf16)


def fill(out, unit, start, count, picks):
    low = low_lanes((8, 128))
    for half in range(2):
        rows = jnp.where(low, picks[2 * half], picks[2 * half + 1])
        for k in range(count):
            row = jnp.broadcast_to(rows[k : k + 1], (16, 128)).astype(bf16)
            block = jnp.concatenate([row] * (GROUP // 16)) * unit
            place = start + k * TILE
            out[place : place + GROUP, half * 128 : half * 128 + 128] = block


def zonal_matrix(out, unit, g, rows, count):
    for i in range(PLACES):
        for m in range(count // 8):
            base = [32 * m + 8 * (i - o) + 24 for o in range(PLACES)]
            fill(out, unit, m * 8 * TILE + i * GROUP, 8, [rows[g, k : k + 8] for k in base])


def local_matrix(out, unit, g, rows, blocks, start=0):
    for b in blocks:
        for i in range(PLACES):
            base = [4 * (b - 1) + i - o + RIM + 4 for o in range(PLACES)]
            fill(out, unit, start + i * GROUP, 7, [rows[g, k] for k in base])
        start += 7 * TILE


def pair_columns(wide, pairs, length):
    low = low_lanes((length, 128))
    for r in range(ROWS):
        value = wide[r, 0 : length + 8]
        turned = swap_halves(value)
        pairs[0, r] = jnp.where(low, value[:length], turned[8:])
        pairs[1, r] = jnp.where(low, turned[:length], value[8:])
    for r in range(16):
        value = wide[32 + r, 0 : length + 8]
        turned = swap_halves(value)
        pairs[2, r] = jnp.where(low, value[:length], turned[8:])
        pairs[2, 16 + r] = jnp.where(low, turned[:length], value[8:])


def zonal_product(g, pairs, left, rows, matrix, count):
    zonal_matrix(matrix, units(), g, rows, count)
    for tile in range(count):
        start = tile % 8 + 32 * (tile // 8)
        for half in range(2):
            value = pairs[g, :, start + 16 * half : start + 16 * half + 8, :]
            column = tile * TILE + half * 128
            left[:, column : column + 128] = value.reshape(CHUNK, 128).astype(bf16)
    return jnp.dot(left[...], matrix[0 : count * TILE], preferred_element_type=f32)


def near_body(block_odd, own, inner, rows, out, wide, pairs, left, matrix, arrive):
    odd = block_odd[0] == 1
    for r in range(48):
        wide[r, 0:8] = jnp.zeros((8, 128), f32)
        wide[r, 56:72] = jnp.zeros((16, 128), f32)

    @pl.when(odd)
    def _():
        for r in range(48):
            wide[r, 0:32] = inner[r].astype(f32)
            wide[r, 30:62] = own[r].astype(f32)

    @pl.when(jnp.logical_not(odd))
    def _():
        for r in range(48):
            wide[r, 7:39] = own[r].astype(f32)
            wide[r, 37:69] = inner[r].astype(f32)

    pair_columns(wide, pairs, 64)
    arrive(0)

    @pl.loop(0, GROUPS)
    def _(g):
        out[g] = zonal_product(g, pairs, left, rows, matrix, 16)


def rims_body(block_odd, flags, own, inner, outer, near_out, far_out, rim):
    odd, upper, top = block_odd[0] == 1, flags[0] == 1, flags[2] == 1
    places = list(range(3)) + list(range(32, 35)) + list(range(29, 32)) + list(range(45, 48))
    for k, r in enumerate(places):
        ins, outs = inner[r].astype(f32), outer[r].astype(f32)
        west, east = jnp.where(odd, ins, outs), jnp.where(odd, outs, ins)
        rim[k, 3:35] = own[r].astype(f32)
        rim[k, 0:3] = west[27:30]
        rim[k, 33:36] = east[0:3]
        rim[k, 36:40] = jnp.zeros((4, 128), f32)
    place = lax.broadcasted_iota(jnp.int32, (40, 40), 0)
    mirror = place + lax.broadcasted_iota(jnp.int32, (40, 40), 1) == COLS + 2 * RIM - 1
    mirror = jnp.where(mirror, 1.0, 0.0).astype(bf16)
    for k in range(6):
        low, high = rim[k], rim[6 + k]
        near_out[k] = jnp.where(upper, low, high).astype(bf16)
        far_out[k] = jnp.where(upper, high, low).astype(bf16)

    @pl.when(top)
    def _():
        for k in range(6):
            value = rim[8 - k] if k < 3 else swap_halves(rim[14 - k])
            turned = jnp.dot(mirror, value.astype(bf16), preferred_element_type=f32)
            far_out[k] = turned.astype(bf16)


def inner_body(
    block_odd, own, inner, outer, zonal, far, local, zonal_out, local_out,
    wide, pairs, field, row_pairs, zonal_left, local_left, matrix, arrive,
):
    odd = block_odd[0] == 1
    for r in range(48):
        wide[r] = jnp.zeros((48, 128), f32)

    @pl.when(odd)
    def _():
        for r in range(48):
            wide[r, 7:39] = outer[r].astype(f32)

    @pl.when(jnp.logical_not(odd))
    def _():
        for r in range(48):
            wide[r, 0:32] = outer[r].astype(f32)

    pair_columns(wide, pairs, 40)
    for r in range(48):
        ins, outs = inner[r].astype(f32), outer[r].astype(f32)
        west, east = jnp.where(odd, ins, outs), jnp.where(odd, outs, ins)
        field[r, 8:40] = own[r].astype(f32)
        field[r, 5:8] = west[27:30]
        field[r, 38:46] = east[0:8]
    low = low_lanes((48, 128))
    for q in range(16):
        first, second = field[2 * q], field[2 * q + 1]
        row_pairs[0, q] = jnp.where(low, first, swap_halves(second))
        row_pairs[1, q] = jnp.where(low, swap_halves(first), second)
        first, second = field[32 + 2 * q % 16], field[33 + 2 * q % 16]
        if q < 8:
            row_pairs[2, q] = jnp.where(low, first, swap_halves(second))
        else:
            row_pairs[2, q] = jnp.where(low, swap_halves(first), second)
    depth = 7 * TILE
    arrive(0)
    arrive(1)

    @pl.loop(0, GROUPS)
    def _(g):
        zonal_out[g] = zonal[g] + zonal_product(g, pairs, zonal_left, far, matrix, 8)
        local_matrix(matrix, units(), g, local, range(3))
        for shift in range(7):
            for half in range(2):
                column = shift * TILE + half * 128
                for block in range(8):
                    value = row_pairs[g, 2 * block + half, 5 + shift : 37 + shift, :]
                    local_left[block * 32 : block * 32 + 32, column : column + 128] = (
                        value.astype(bf16)
                    )
        local_out[g] = jnp.dot(
            local_left[...], matrix[depth : 2 * depth], preferred_element_type=f32
        )
        local_out[g, 32:256] += jnp.dot(
            local_left[0:224], matrix[0:depth], preferred_element_type=f32
        )
        local_out[g, 0:224] += jnp.dot(
            local_left[32:256], matrix[2 * depth : 3 * depth], preferred_element_type=f32
        )


def edges(band_odd, near_rows, far_rows, local, north, edge, rim, row_pairs, left, matrix, arrive):
    upper, bottom = band_odd[0] == 1, band_odd[1] == 1
    low = low_lanes((48, 128))
    nothing = jnp.zeros((48, 128), f32)
    for k in range(6):
        near, far = near_rows[k].astype(f32), far_rows[k].astype(f32)
        rim[k, 5:45] = jnp.where(upper, near, jnp.where(bottom, jnp.zeros_like(far), far))
        rim[6 + k, 5:45] = jnp.where(upper, far, near)
    below = [(nothing, nothing)] + [(rim[k], rim[3 + k]) for k in range(3)]
    above = [(rim[6 + k], rim[9 + k]) for k in range(3)] + [(nothing, nothing)]
    for side, rows in enumerate((below, above)):
        for half in range(2):
            (a, c), (b, d) = rows[2 * half], rows[2 * half + 1]
            place = 2 * side + half
            row_pairs[0, place] = jnp.where(low, a, swap_halves(b))
            row_pairs[1, place] = jnp.where(low, swap_halves(a), b)
            if side == 0:
                row_pairs[2, place] = jnp.where(low, swap_halves(c), d)
            else:
                row_pairs[2, place] = jnp.where(low, c, swap_halves(d))

    arrive(0)
    arrive(1)

    @pl.loop(0, GROUPS)
    def _(g):
        for side in range(2):
            for shift in range(7):
                for half in range(2):
                    column = shift * TILE + half * 128
                    value = row_pairs[g, 2 * side + half, 5 + shift : 37 + shift, :]
                    left[side * 32 : side * 32 + 32, column : column + 128] = value.astype(bf16)
        unit, depth = units(), 7 * TILE
        local_matrix(matrix, unit, g, local, (0,))
        local_matrix(matrix, unit, g, north, (2,), depth)
        edge[g, 0:32] = jnp.dot(left[0:32], matrix[0:depth], preferred_element_type=f32)
        edge[g, 32:64] = jnp.dot(
            left[32:64], matrix[depth : 2 * depth], preferred_element_type=f32
        )


def mixed_rows(row, zonal_out, local_out, edge):
    block, place = row // PLACES, row % PLACES

    def joined(first, second, third, odd):
        mask = low_lanes(first.shape)
        if odd:
            return jnp.where(mask, swap_halves(first), second), swap_halves(third)
        return jnp.where(mask, first, swap_halves(second)), third

    lanes = slice(place // 2 * 128, place // 2 * 128 + 128)
    parts = [local_out[g, block * 32 : block * 32 + 32, lanes] for g in range(GROUPS)]
    if block == 0:
        parts = [parts[g] + edge[g, 0:32, lanes] for g in range(GROUPS)]
    if block == ROWS // PLACES - 1:
        parts = [parts[g] + edge[g, 32:64, lanes] for g in range(GROUPS)]
    local_a, local_b = joined(*parts, place % 2)
    zonal_a, zonal_b = [], []
    for spot in range(PLACES):
        lanes = slice(spot // 2 * 128, spot // 2 * 128 + 128)
        parts = [zonal_out[g, row * 8 : row * 8 + 8, lanes] for g in range(GROUPS)]
        first, second = joined(*parts, spot % 2)
        zonal_a.append(first)
        zonal_b.append(second)
    zonal_a, zonal_b = jnp.concatenate(zonal_a), jnp.concatenate(zonal_b)
    a = local_a + zonal_a.astype(bf16).astype(f32)
    b = local_b + zonal_b.astype(bf16).astype(f32)
    return a, b


def store_mixture(mixture, *parts):
    for row in range(ROWS):
        a, b = mixed_rows(row, *parts)
        mixture[row * WIDE : (row + 1) * WIDE, 0:128] = a
        mixture[row * WIDE : (row + 1) * WIDE, 128:256] = b


def store_packed(field, packed):
    low = low_lanes((WIDE, 128))
    for row in range(ROWS):
        packed[row] = field[row * WIDE : (row + 1) * WIDE, 0:128].astype(bf16)
    for row in range(16):
        first = field[row * WIDE : (row + 1) * WIDE, 128:256]
        second = field[(row + 16) * WIDE : (row + 17) * WIDE, 128:256]
        packed[ROWS + row] = jnp.where(low, first, swap_halves(second)).astype(bf16)


def normalized(value, gain):
    average = jnp.mean(value, axis=-1, keepdims=True)
    centered = value - average
    variance = jnp.mean(centered * centered, axis=-1, keepdims=True)
    inverse = lax.rsqrt(variance + epsilon)
    unit = centered * inverse
    return unit, inverse, (unit * gain).astype(bf16)


def gelu_parts(value):
    square = value * value
    bent = jnp.tanh(gelu_scale * value * (1.0 + gelu_cube * square))
    share = 0.5 + 0.5 * bent
    return square, bent, share


def transposed_dot(left, right):
    return lax.dot_general(left, right, (((1,), (1,)), ((), ())), preferred_element_type=f32)


def backward(rows, mixture, adjoint, weight, gain, weight_in, weight_out, field, saved):
    normed_out, hidden_out, preact_out, update_out = saved
    unit, inverse, normed = normalized(mixture, gain)
    preact = jnp.dot(normed, weight_in[...], preferred_element_type=f32)
    square, bent, share = gelu_parts(preact)
    update = (weight * adjoint).astype(bf16)
    slope = share + 0.5 * preact * (1.0 - bent * bent) * gelu_scale * (
        1.0 + 3.0 * gelu_cube * square
    )
    grad_preact = (jnp.dot(update, weight_out[...], preferred_element_type=f32) * slope).astype(bf16)
    normed_out[rows] = normed
    hidden_out[rows] = (preact * share).astype(bf16)
    preact_out[rows] = grad_preact
    update_out[rows] = update
    grad = transposed_dot(grad_preact, weight_in[...]) * gain
    shared = jnp.mean(grad, axis=-1, keepdims=True)
    along = jnp.mean(grad * unit, axis=-1, keepdims=True)
    field[rows, 0:CHANNELS] = inverse * (grad - shared - unit * along)


def first_step(
    flags, near_rows, far_rows, zonal, inner, weight_ref, state, gain, weight_in, weight_out,
    local, north, packed, mixture_out, field, *scratch, arrive, send, sent,
):
    edges(flags, near_rows, far_rows, local, north, *scratch, arrive)
    store_mixture(field, zonal, inner, scratch[0])

    @pl.loop(0, CELLS // CHUNK)
    def _(chunk):
        rows = pl.ds(pl.multiple_of(chunk * CHUNK, CHUNK), CHUNK)
        mixture = field[rows, 0:CHANNELS]
        mixture_out[rows] = mixture
        send(0, rows, chunk)
        normed = normalized(mixture, gain[...])[2]
        preact = jnp.dot(normed, weight_in[...], preferred_element_type=f32)
        hidden = (preact * gelu_parts(preact)[2]).astype(bf16)
        update = transposed_dot(hidden, weight_out[...])
        weight = weight_ref[rows].astype(f32)
        field[rows, 0:CHANNELS] = weight * (state[rows].astype(f32) + update)

    store_packed(field, packed)
    for chunk in range(CELLS // CHUNK):
        sent(0, slice(chunk * CHUNK, (chunk + 1) * CHUNK), chunk)


def second_step(
    flags, near_rows, far_rows, zonal, inner, weight_ref, cotangent, gain, weight_in, weight_out,
    local, north, packed, totals, normed, hidden, grad_preact, update, field, *scratch,
    arrive, send, sent,
):
    saved = normed, hidden, grad_preact, update
    edges(flags, near_rows, far_rows, local, north, *scratch, arrive)
    store_mixture(field, zonal, inner, scratch[0])

    @pl.loop(0, CELLS // CHUNK)
    def _(chunk):
        rows = pl.ds(pl.multiple_of(chunk * CHUNK, CHUNK), CHUNK)
        backward(
            rows,
            field[rows, 0:CHANNELS],
            cotangent[rows].astype(f32),
            weight_ref[rows].astype(f32),
            gain[...],
            weight_in,
            weight_out,
            field,
            saved,
        )

    store_totals(*saved, totals)
    send(0, slice(0, 2), 0)
    store_packed(field, packed)
    sent(0, slice(0, 2), 0)


def third_step(
    flags, near_rows, far_rows, zonal, inner, weight_ref, cotangent, gain, weight_in, weight_out,
    local, north, mixture_in, before, packed, totals, adjoint_out,
    normed, hidden, grad_preact, update, field, *scratch, arrive, send, sent,
):
    saved = normed, hidden, grad_preact, update
    edges(flags, near_rows, far_rows, local, north, *scratch, arrive)
    store_mixture(field, zonal, inner, scratch[0])
    arrive(2)
    arrive(3)

    @pl.loop(0, CELLS // CHUNK)
    def _(chunk):
        rows = pl.ds(pl.multiple_of(chunk * CHUNK, CHUNK), CHUNK)
        weight = weight_ref[rows].astype(f32)
        adjoint = weight * cotangent[rows].astype(f32) + field[rows, 0:CHANNELS]
        adjoint_out[rows] = adjoint
        send(0, rows, chunk)
        backward(
            rows, mixture_in[rows], adjoint, weight, gain[...], weight_in, weight_out, field, saved
        )

    store_totals(*saved, totals, before)
    store_packed(field, packed)
    for chunk in range(CELLS // CHUNK):
        sent(0, slice(chunk * CHUNK, (chunk + 1) * CHUNK), chunk)


def last_step(
    flags, near_rows, far_rows, zonal, inner, weight_ref, local, north, adjoint, out, *scratch,
    arrive,
):
    edges(flags, near_rows, far_rows, local, north, *scratch, arrive)
    arrive(2)
    for row in range(ROWS):
        cells = slice(row * WIDE, (row + 1) * WIDE)
        a, b = mixed_rows(row, zonal, inner, scratch[0])
        weight, value = weight_ref[cells].astype(f32), adjoint[cells]
        kept = weight * value
        out[row, :, 0:128] = (kept[:, :128] + a)[:COLS]
        out[row, :, 128:CHANNELS] = (kept[:, 128:] + b[:, : CHANNELS - 128])[:COLS]


def column_dot(left, right):
    return lax.dot_general(left, right, (((0,), (0,)), ((), ())), preferred_element_type=f32)


def store_totals(normed, hidden, grad_preact, update, out, before=None):
    for index, (left, right) in enumerate(((normed, grad_preact), (update, hidden))):
        product = column_dot(left[...], right[...])
        for k in range(HIDDEN // 128):
            rows = slice(k * CHANNELS, (k + 1) * CHANNELS)
            part = product[:, k * 128 : (k + 1) * 128]
            out[index, rows] = part if before is None else before[index, rows] + part


def packing(state, packed, field):
    for row in range(ROWS):
        field[row * WIDE : (row + 1) * WIDE, 0:CHANNELS] = state[
            row * WIDE : (row + 1) * WIDE
        ].astype(f32)
    store_packed(field, packed)


PARTS = [
    pltpu.VMEM((GROUPS, 64, TILE), f32),
    pltpu.VMEM((12, 48, 128), f32),
    pltpu.VMEM((GROUPS, 4, 48, 128), f32),
    pltpu.VMEM((64, 7 * TILE), bf16),
    pltpu.VMEM((14 * TILE, TILE), bf16),
]
FIELD = [pltpu.VMEM((CELLS, 256), f32)]


def shape(dims, dtype):
    return jax.ShapeDtypeStruct(dims, dtype)


def run(body, outs, scalars, args, scratch, name, us=1.0, after=(), late=(), far_outs=()):
    vmem, hbm = pl.BlockSpec(memory_space=pltpu.VMEM), pl.BlockSpec(memory_space=pltpu.HBM)
    sizes = [len(scalars), len(args), len(late), len(after), len(outs), len(far_outs)]
    sizes += [len(late), len(far_outs)]

    def called(*refs):
        groups, start = [], 0
        for size in sizes:
            groups.append(refs[start : start + size])
            start += size
        numbers, ins, sources, _, results, targets, fetched, staged = groups
        rest = refs[start:]
        options = {}
        if late:
            arrivals, rest = rest[0], rest[1:]
            copies = [
                pltpu.make_async_copy(source, place, arrivals.at[i])
                for i, (source, place) in enumerate(zip(sources, fetched))
            ]
            for copy in copies:
                copy.start()
            options["arrive"] = lambda i: copies[i].wait()
        if far_outs:
            departures, rest = rest[0], rest[1:]

            def leaving(i, rows, slot):
                return pltpu.make_async_copy(
                    staged[i].at[rows], targets[i].at[rows], departures.at[slot]
                )

            options["send"] = lambda i, rows, slot: leaving(i, rows, slot).start()
            options["sent"] = lambda i, rows, slot: leaving(i, rows, slot).wait()
        body(*numbers, *ins, *fetched, *results, *staged, *rest, **options)

    extra = [pltpu.VMEM(x.shape, x.dtype) for x in (*late, *far_outs)]
    if late:
        extra.append(pltpu.SemaphoreType.DMA((len(late),)))
    if far_outs:
        extra.append(pltpu.SemaphoreType.DMA((8,)))
    return pl.pallas_call(
        called,
        out_shape=[*outs, *far_outs],
        in_specs=[pl.BlockSpec(memory_space=pltpu.SMEM)] * len(scalars)
        + [vmem] * len(args)
        + [hbm] * len(late)
        + [pl.BlockSpec(memory_space=pl.ANY)] * len(after),
        out_specs=[vmem] * len(outs) + [hbm] * len(far_outs),
        scratch_shapes=extra + scratch,
        compiler_params=pltpu.CompilerParams(vmem_limit_bytes=VMEM_LIMIT),
        cost_estimate=pl.CostEstimate(
            flops=int(us * 1.1e9), bytes_accessed=int(us * 1e6), transcendentals=0
        ),
        name=name,
    )(*scalars, *args, *late, *after)


PACKED = [shape((48, WIDE, 128), bf16)]
SAVED = [
    pltpu.VMEM((CELLS, CHANNELS), bf16),
    pltpu.VMEM((CELLS, HIDDEN), bf16),
    pltpu.VMEM((CELLS, HIDDEN), bf16),
    pltpu.VMEM((CELLS, CHANNELS), bf16),
]


def flat_cells(block):
    padded = jnp.pad(block, ((0, 0), (0, WIDE - COLS), (0, 0)))
    return padded.reshape(CELLS, -1)


TOTALS = shape((2, HIDDEN // 128 * CHANNELS, 128), f32)
ZONAL = shape((GROUPS, CHUNK, TILE), f32)
RIMS = shape((6, 40, 128), bf16)
def filtered(packed, odds, rows, ready=()):
    block_odd, band_odd = odds
    near, far, local, north = rows
    inner, outer = block_swaps(packed)
    (zonal,) = run(
        near_body,
        [ZONAL],
        (block_odd,),
        (packed, inner),
        [
            pltpu.VMEM((48, 72, 128), f32),
            pltpu.VMEM((GROUPS, ROWS, 64, 128), f32),
            pltpu.VMEM((CHUNK, 16 * TILE), bf16),
            pltpu.VMEM((16 * TILE, TILE), bf16),
        ],
        "near_zonal",
        4.0,
        after=ready,
        late=(near,),
    )
    rims = run(
        rims_body,
        [RIMS] * 2,
        odds,
        (packed, inner, outer),
        [pltpu.VMEM((12, 40, 128), f32)],
        "rims",
        0.3,
        after=(zonal,),
    )
    near_rows, far_rows = rim_swaps(*rims)
    zonal, mixed = run(
        inner_body,
        [ZONAL, ZONAL],
        (block_odd,),
        (packed, inner, outer, zonal),
        [
            pltpu.VMEM((48, 48, 128), f32),
            pltpu.VMEM((GROUPS, ROWS, 40, 128), f32),
            pltpu.VMEM((48, 48, 128), f32),
            pltpu.VMEM((GROUPS, 16, 48, 128), f32),
            pltpu.VMEM((CHUNK, 8 * TILE), bf16),
            pltpu.VMEM((CHUNK, 7 * TILE), bf16),
            pltpu.VMEM((LOCAL_TILES * TILE, TILE), bf16),
        ],
        "inner_filters",
        5.0,
        late=(far, local),
    )
    return (near_rows, far_rows, zonal, mixed), (local, north)


def shards(
    ocean_state, ocean_mask, cotangent, kernel, zonal_taps, norm_gain, weight_in, weight_out
):
    band = lax.axis_index("band")
    at_top = band == lax.axis_size("band") - 1
    block_odd = lax.axis_index("blk") % 2
    odds = (
        block_odd.astype(jnp.int32).reshape(1),
        jnp.stack([band % 2, (band == 0).astype(jnp.int32), at_top.astype(jnp.int32)]),
    )
    state = flat_cells(ocean_state)
    (packed,) = run(packing, PACKED, (), (state,), FIELD, "packing")
    weight = flat_cells(jnp.broadcast_to(ocean_mask[:, :, None].astype(bf16), ocean_state.shape))
    cells = flat_cells(cotangent)
    mlp = (norm_gain[None], weight_in, weight_out.T)
    zonal_forth = zonal_rows(zonal_taps, block_odd == 1)
    zonal_back = zonal_rows(zonal_taps[::-1], block_odd == 1)
    local_forth, local_back = local_rows(kernel), local_rows(kernel[::-1, ::-1])
    north_back = jnp.where(at_top, local_forth, local_back)
    forth = (*zonal_forth, local_forth, local_forth)
    back = (*zonal_back, local_back, north_back)
    parts = filtered(packed, odds, forth, (weight, *back))
    parts, coefficients = parts
    cell_array = shape((CELLS, CHANNELS), f32)
    packed, mixture = run(
        first_step,
        PACKED,
        odds[1:],
        (*parts, weight, state, *mlp),
        FIELD + PARTS,
        "first_step",
        5.0,
        late=coefficients,
        far_outs=[cell_array],
    )
    parts, coefficients = filtered(packed, odds, forth, (cells,))
    packed, totals = run(
        second_step,
        PACKED,
        odds[1:],
        (*parts, weight, cells, *mlp),
        SAVED + FIELD + PARTS,
        "second_step",
        7.0,
        late=coefficients,
        far_outs=[TOTALS],
    )
    parts, coefficients = filtered(packed, odds, back)
    packed, totals, adjoint = run(
        third_step,
        PACKED + [TOTALS],
        odds[1:],
        (*parts, weight, cells, *mlp),
        SAVED + FIELD + PARTS,
        "third_step",
        7.0,
        late=(*coefficients, mixture, totals),
        far_outs=[cell_array],
    )
    parts, coefficients = filtered(packed, odds, back)
    (grad_state,) = run(
        last_step,
        [shape((ROWS, COLS, CHANNELS), f32)],
        odds[1:],
        (*parts, weight),
        PARTS,
        "last_step",
        3.0,
        late=(*coefficients, adjoint),
    )
    sums = summed(totals)
    cell_count = ROWS * lax.axis_size("band") * COLS * lax.axis_size("blk")
    scaling = 1.0 / math.sqrt(cell_count)
    whole = shape((CHANNELS, HIDDEN), f32)

    def scaled(sums_ref, in_out, out_out):
        for k in range(HIDDEN // 128):
            for out, index in ((in_out, 0), (out_out, 1)):
                value = sums_ref[index, k * CHANNELS : (k + 1) * CHANNELS].astype(f32)
                out[:, k * 128 : (k + 1) * 128] = value * scaling

    grad_in, grad_out = run(scaled, [whole, whole], (), (sums,), [], "scaled", 0.5)
    return (grad_state, grad_in, grad_out.T)


def solution(mesh):
    return jax.shard_map(
        shards,
        mesh=mesh,
        in_specs=(
            P("band", "blk", None),
            P("band", "blk"),
            P("band", "blk", None),
            P(),
            P(),
            P(),
            P(),
            P(),
        ),
        out_specs=(P("band", "blk", None), P(), P()),
        check_vma=False,
    )
```

```python
import math

import jax
import jax.numpy as jnp
from jax import lax
from jax.experimental import pallas as pl
from jax.experimental.pallas import tpu as pltpu
from jax.sharding import PartitionSpec as P

ROWS, COLS, CHANNELS, HIDDEN = 32, 30, 192, 768
WIDE = 32
CELLS = ROWS * WIDE
RIM, HALF, GROUP, GROUPS, PLACES = 3, 30, 64, 3, 4
ZONAL_TILES, LOCAL_TILES = 24, 21
TILE = GROUP * PLACES
CHUNK = 256
VMEM_LIMIT = 24 * 2**20
bf16, f32 = jnp.bfloat16, jnp.float32
epsilon = 1e-06
gelu_scale, gelu_cube = math.sqrt(2.0 / math.pi), 0.044715


def ways(axis, low, count):
    position = (lax.axis_index(axis) // low) % count
    pairs = [
        [(i, i ^ (low * step)) for i in range(lax.axis_size(axis))] for step in range(count)
    ]
    return position, pairs


def plus_body(*refs):
    total = refs[0][...].astype(f32)
    for ref in refs[1:-1]:
        total = total + ref[...].astype(f32)
    refs[-1][...] = total.astype(refs[-1].dtype)


def split_body(position, kept, arrived, own, first, second, third, total):
    total[...] = kept[...] + arrived[...].astype(f32)
    own[...] = total[position[0]]
    for step, out in ((1, first), (2, second), (3, third)):
        out[...] = total[position[0] ^ step].astype(bf16)


def join_body(position, own, first, second, third, out):
    for step, value in enumerate((own, first, second, third)):
        out[position[0] ^ step] = value[...]


def summed(kept, sent, zonal, rim, mixed, final):
    blocks = range(lax.axis_size("blk"))
    cores = [(i, i ^ 1) for i in blocks]
    position, pairs = ways("blk", 2, 4)
    position = position.astype(jnp.int32).reshape(1)
    piece, wide_piece = shape(sent.shape[1:], bf16), shape(sent.shape[1:], f32)
    arrived = lax.ppermute(sent, "blk", cores)
    own, *others = run(
        split_body,
        [wide_piece] + [piece] * 3,
        (position,),
        (kept, arrived),
        [pltpu.VMEM(kept.shape, f32)],
        "split",
        0.3,
    )
    others = [lax.ppermute(others[k - 1], "blk", pairs[k]) for k in (1, 2, 3)]
    (value,) = run(plus_body, [piece], (), (own, *others), [], "sum_y", 0.2, after=(zonal,))
    stages = (
        ("blk", 8, (rim,)),
        ("blk", 24, ()),
        ("band", 1, (mixed,)),
        ("band", 2, (final,)),
        ("band", 6, ()),
    )
    for axis, step, after in stages:
        other = lax.ppermute(value, axis, [(i, i ^ step) for i in range(lax.axis_size(axis))])
        (value,) = run(plus_body, [piece], (), (value, other), [], f"sum_{axis}{step}", 0.2, after)
    others = [lax.ppermute(value, "blk", pairs[k]) for k in (1, 2, 3)]
    half = shape(sent.shape, bf16)
    (half,) = run(join_body, [half], (position,), (value, *others), [], "join", 0.2)
    return half, lax.ppermute(half, "blk", cores)


def block_swaps(packed):
    blocks = lax.axis_size("blk")
    inner = [(i, i ^ 1) for i in range(blocks)]
    outer = [(i, (i + 1) % blocks if i % 2 else (i - 1) % blocks) for i in range(blocks)]
    return lax.ppermute(packed, "blk", inner), lax.ppermute(packed, "blk", outer)


def rim_swaps(to_near, to_far):
    bands, blocks = lax.axis_size("band"), lax.axis_size("blk")
    near = [
        (b * blocks + i, (b ^ 1) * blocks + i) for b in range(bands) for i in range(blocks)
    ]
    far = [
        (b * blocks + i, (b + 1 if b % 2 else b - 1) * blocks + i)
        for b in range(1, bands - 1)
        for i in range(blocks)
    ]
    last = (bands - 1) * blocks
    far += [(last + i, last + blocks - 1 - i) for i in range(blocks)]
    far += [(i, i ^ 1) for i in range(blocks)]
    return (
        lax.ppermute(to_near, ("band", "blk"), near),
        lax.ppermute(to_far, ("band", "blk"), far),
    )


def zonal_rows(taps, odd_block):
    padded = jnp.pad(taps.astype(f32), ((24, 27), (0, 0))).reshape(-1, GROUPS, GROUP)
    padded = jnp.swapaxes(padded, 0, 1)
    padded = jnp.concatenate([padded, padded], axis=2)
    near = jnp.where(odd_block, padded[:, 0:88], padded[:, 23:111])
    far = jnp.where(odd_block, padded[:, 53:109], padded[:, 0:56])
    return near, far


def local_rows(kernel):
    padded = jnp.pad(kernel.astype(f32), ((4, 4), (0, 1), (0, 0)))
    padded = padded.reshape(15, 8, GROUPS, GROUP).transpose(2, 0, 1, 3)
    return jnp.concatenate([padded, padded], axis=3)


def low_lanes(shape):
    return lax.broadcasted_iota(jnp.int32, shape, len(shape) - 1) < GROUP


def swap_halves(value):
    return pltpu.roll(value, GROUP, value.ndim - 1)


def units():
    same = (
        lax.broadcasted_iota(jnp.int32, (GROUP, 128), 0)
        == lax.broadcasted_iota(jnp.int32, (GROUP, 128), 1) % GROUP
    )
    return jnp.where(same, 1.0, 0.0).astype(bf16)


def fill(out, unit, start, count, picks):
    low = low_lanes((8, 128))
    for half in range(2):
        rows = jnp.where(low, picks[2 * half], picks[2 * half + 1])
        for k in range(count):
            row = jnp.broadcast_to(rows[k : k + 1], (16, 128)).astype(bf16)
            block = jnp.concatenate([row] * (GROUP // 16)) * unit
            place = start + k * TILE
            out[place : place + GROUP, half * 128 : half * 128 + 128] = block


def zonal_matrix(out, unit, g, rows, count):
    for i in range(PLACES):
        for m in range(count // 8):
            base = [32 * m + 8 * (i - o) + 24 for o in range(PLACES)]
            fill(out, unit, m * 8 * TILE + i * GROUP, 8, [rows[g, k : k + 8] for k in base])


def local_matrix(out, unit, g, rows, blocks, start=0):
    for b in blocks:
        for i in range(PLACES):
            base = [4 * (b - 1) + i - o + RIM + 4 for o in range(PLACES)]
            fill(out, unit, start + i * GROUP, 7, [rows[g, k] for k in base])
        start += 7 * TILE


def pair_columns(wide, pairs, length):
    low = low_lanes((length, 128))
    for r in range(ROWS):
        value = wide[r, 0 : length + 8]
        turned = swap_halves(value)
        pairs[0, r] = jnp.where(low, value[:length], turned[8:])
        pairs[1, r] = jnp.where(low, turned[:length], value[8:])
    for r in range(16):
        value = wide[32 + r, 0 : length + 8]
        turned = swap_halves(value)
        pairs[2, r] = jnp.where(low, value[:length], turned[8:])
        pairs[2, 16 + r] = jnp.where(low, turned[:length], value[8:])


def zonal_product(g, pairs, left, rows, matrix, count):
    zonal_matrix(matrix, units(), g, rows, count)
    for tile in range(count):
        start = tile % 8 + 32 * (tile // 8)
        for half in range(2):
            value = pairs[g, :, start + 16 * half : start + 16 * half + 8, :]
            column = tile * TILE + half * 128
            left[:, column : column + 128] = value.reshape(CHUNK, 128).astype(bf16)
    return jnp.dot(left[...], matrix[0 : count * TILE], preferred_element_type=f32)


def near_body(block_odd, own, inner, rows, out, wide, pairs, left, matrix, arrive):
    odd = block_odd[0] == 1
    for r in range(48):
        wide[r, 0:8] = jnp.zeros((8, 128), f32)
        wide[r, 56:72] = jnp.zeros((16, 128), f32)

    @pl.when(odd)
    def _():
        for r in range(48):
            wide[r, 0:32] = inner[r].astype(f32)
            wide[r, 30:62] = own[r].astype(f32)

    @pl.when(jnp.logical_not(odd))
    def _():
        for r in range(48):
            wide[r, 7:39] = own[r].astype(f32)
            wide[r, 37:69] = inner[r].astype(f32)

    pair_columns(wide, pairs, 64)
    arrive(0)

    @pl.loop(0, GROUPS)
    def _(g):
        out[g] = zonal_product(g, pairs, left, rows, matrix, 16)


def rims_body(block_odd, flags, own, inner, outer, near_out, far_out, rim):
    odd, upper, top = block_odd[0] == 1, flags[0] == 1, flags[2] == 1
    places = list(range(3)) + list(range(32, 35)) + list(range(29, 32)) + list(range(45, 48))
    for k, r in enumerate(places):
        ins, outs = inner[r].astype(f32), outer[r].astype(f32)
        west, east = jnp.where(odd, ins, outs), jnp.where(odd, outs, ins)
        rim[k, 3:35] = own[r].astype(f32)
        rim[k, 0:3] = west[27:30]
        rim[k, 33:36] = east[0:3]
        rim[k, 36:40] = jnp.zeros((4, 128), f32)
    place = lax.broadcasted_iota(jnp.int32, (40, 40), 0)
    mirror = place + lax.broadcasted_iota(jnp.int32, (40, 40), 1) == COLS + 2 * RIM - 1
    mirror = jnp.where(mirror, 1.0, 0.0).astype(bf16)
    for k in range(6):
        low, high = rim[k], rim[6 + k]
        near_out[k] = jnp.where(upper, low, high).astype(bf16)
        far_out[k] = jnp.where(upper, high, low).astype(bf16)

    @pl.when(top)
    def _():
        for k in range(6):
            value = rim[8 - k] if k < 3 else swap_halves(rim[14 - k])
            turned = jnp.dot(mirror, value.astype(bf16), preferred_element_type=f32)
            far_out[k] = turned.astype(bf16)


def inner_body(
    block_odd, own, inner, outer, zonal, far, local, zonal_out, local_out,
    wide, pairs, field, row_pairs, zonal_left, local_left, matrix, arrive,
):
    odd = block_odd[0] == 1
    for r in range(48):
        wide[r] = jnp.zeros((48, 128), f32)

    @pl.when(odd)
    def _():
        for r in range(48):
            wide[r, 7:39] = outer[r].astype(f32)

    @pl.when(jnp.logical_not(odd))
    def _():
        for r in range(48):
            wide[r, 0:32] = outer[r].astype(f32)

    pair_columns(wide, pairs, 40)
    for r in range(48):
        ins, outs = inner[r].astype(f32), outer[r].astype(f32)
        west, east = jnp.where(odd, ins, outs), jnp.where(odd, outs, ins)
        field[r, 8:40] = own[r].astype(f32)
        field[r, 5:8] = west[27:30]
        field[r, 38:46] = east[0:8]
    low = low_lanes((48, 128))
    for q in range(16):
        first, second = field[2 * q], field[2 * q + 1]
        row_pairs[0, q] = jnp.where(low, first, swap_halves(second))
        row_pairs[1, q] = jnp.where(low, swap_halves(first), second)
        first, second = field[32 + 2 * q % 16], field[33 + 2 * q % 16]
        if q < 8:
            row_pairs[2, q] = jnp.where(low, first, swap_halves(second))
        else:
            row_pairs[2, q] = jnp.where(low, swap_halves(first), second)
    depth = 7 * TILE
    arrive(0)
    arrive(1)

    @pl.loop(0, GROUPS)
    def _(g):
        zonal_out[g] = zonal[g] + zonal_product(g, pairs, zonal_left, far, matrix, 8)
        local_matrix(matrix, units(), g, local, range(3))
        for shift in range(7):
            for half in range(2):
                column = shift * TILE + half * 128
                for block in range(8):
                    value = row_pairs[g, 2 * block + half, 5 + shift : 37 + shift, :]
                    local_left[block * 32 : block * 32 + 32, column : column + 128] = (
                        value.astype(bf16)
                    )
        local_out[g] = jnp.dot(
            local_left[...], matrix[depth : 2 * depth], preferred_element_type=f32
        )
        local_out[g, 32:256] += jnp.dot(
            local_left[0:224], matrix[0:depth], preferred_element_type=f32
        )
        local_out[g, 0:224] += jnp.dot(
            local_left[32:256], matrix[2 * depth : 3 * depth], preferred_element_type=f32
        )


def edges(band_odd, near_rows, far_rows, local, north, edge, rim, row_pairs, left, matrix, arrive):
    upper, bottom = band_odd[0] == 1, band_odd[1] == 1
    low = low_lanes((48, 128))
    nothing = jnp.zeros((48, 128), f32)
    for k in range(6):
        near, far = near_rows[k].astype(f32), far_rows[k].astype(f32)
        rim[k, 5:45] = jnp.where(upper, near, jnp.where(bottom, jnp.zeros_like(far), far))
        rim[6 + k, 5:45] = jnp.where(upper, far, near)
    below = [(nothing, nothing)] + [(rim[k], rim[3 + k]) for k in range(3)]
    above = [(rim[6 + k], rim[9 + k]) for k in range(3)] + [(nothing, nothing)]
    for side, rows in enumerate((below, above)):
        for half in range(2):
            (a, c), (b, d) = rows[2 * half], rows[2 * half + 1]
            place = 2 * side + half
            row_pairs[0, place] = jnp.where(low, a, swap_halves(b))
            row_pairs[1, place] = jnp.where(low, swap_halves(a), b)
            if side == 0:
                row_pairs[2, place] = jnp.where(low, swap_halves(c), d)
            else:
                row_pairs[2, place] = jnp.where(low, c, swap_halves(d))

    arrive(0)
    arrive(1)

    @pl.loop(0, GROUPS)
    def _(g):
        for side in range(2):
            for shift in range(7):
                for half in range(2):
                    column = shift * TILE + half * 128
                    value = row_pairs[g, 2 * side + half, 5 + shift : 37 + shift, :]
                    left[side * 32 : side * 32 + 32, column : column + 128] = value.astype(bf16)
        unit, depth = units(), 7 * TILE
        local_matrix(matrix, unit, g, local, (0,))
        local_matrix(matrix, unit, g, north, (2,), depth)
        edge[g, 0:32] = jnp.dot(left[0:32], matrix[0:depth], preferred_element_type=f32)
        edge[g, 32:64] = jnp.dot(
            left[32:64], matrix[depth : 2 * depth], preferred_element_type=f32
        )


def mixed_rows(row, zonal_out, local_out, edge):
    block, place = row // PLACES, row % PLACES

    def joined(first, second, third, odd):
        mask = low_lanes(first.shape)
        if odd:
            return jnp.where(mask, swap_halves(first), second), swap_halves(third)
        return jnp.where(mask, first, swap_halves(second)), third

    lanes = slice(place // 2 * 128, place // 2 * 128 + 128)
    parts = [local_out[g, block * 32 : block * 32 + 32, lanes] for g in range(GROUPS)]
    if block == 0:
        parts = [parts[g] + edge[g, 0:32, lanes] for g in range(GROUPS)]
    if block == ROWS // PLACES - 1:
        parts = [parts[g] + edge[g, 32:64, lanes] for g in range(GROUPS)]
    local_a, local_b = joined(*parts, place % 2)
    zonal_a, zonal_b = [], []
    for spot in range(PLACES):
        lanes = slice(spot // 2 * 128, spot // 2 * 128 + 128)
        parts = [zonal_out[g, row * 8 : row * 8 + 8, lanes] for g in range(GROUPS)]
        first, second = joined(*parts, spot % 2)
        zonal_a.append(first)
        zonal_b.append(second)
    zonal_a, zonal_b = jnp.concatenate(zonal_a), jnp.concatenate(zonal_b)
    a = local_a + zonal_a.astype(bf16).astype(f32)
    b = local_b + zonal_b.astype(bf16).astype(f32)
    return a, b


def store_mixture(mixture, *parts):
    for row in range(ROWS):
        a, b = mixed_rows(row, *parts)
        mixture[row * WIDE : (row + 1) * WIDE, 0:128] = a
        mixture[row * WIDE : (row + 1) * WIDE, 128:256] = b


def store_packed(field, packed):
    low = low_lanes((WIDE, 128))
    for row in range(ROWS):
        packed[row] = field[row * WIDE : (row + 1) * WIDE, 0:128].astype(bf16)
    for row in range(16):
        first = field[row * WIDE : (row + 1) * WIDE, 128:256]
        second = field[(row + 16) * WIDE : (row + 17) * WIDE, 128:256]
        packed[ROWS + row] = jnp.where(low, first, swap_halves(second)).astype(bf16)


def normalized(value, gain):
    average = jnp.mean(value, axis=-1, keepdims=True)
    centered = value - average
    variance = jnp.mean(centered * centered, axis=-1, keepdims=True)
    inverse = lax.rsqrt(variance + epsilon)
    unit = centered * inverse
    return unit, inverse, (unit * gain).astype(bf16)


def gelu_parts(value):
    square = value * value
    bent = jnp.tanh(gelu_scale * value * (1.0 + gelu_cube * square))
    share = 0.5 + 0.5 * bent
    return square, bent, share


def transposed_dot(left, right):
    return lax.dot_general(left, right, (((1,), (1,)), ((), ())), preferred_element_type=f32)


def backward(rows, mixture, adjoint, weight, gain, weight_in, weight_out, field, saved):
    normed_out, hidden_out, preact_out, update_out = saved
    unit, inverse, normed = normalized(mixture, gain)
    preact = jnp.dot(normed, weight_in[...], preferred_element_type=f32)
    square, bent, share = gelu_parts(preact)
    update = (weight * adjoint).astype(bf16)
    slope = share + 0.5 * preact * (1.0 - bent * bent) * gelu_scale * (
        1.0 + 3.0 * gelu_cube * square
    )
    grad_preact = (jnp.dot(update, weight_out[...], preferred_element_type=f32) * slope).astype(bf16)
    normed_out[rows] = normed
    hidden_out[rows] = (preact * share).astype(bf16)
    preact_out[rows] = grad_preact
    update_out[rows] = update
    grad = transposed_dot(grad_preact, weight_in[...]) * gain
    shared = jnp.mean(grad, axis=-1, keepdims=True)
    along = jnp.mean(grad * unit, axis=-1, keepdims=True)
    field[rows, 0:CHANNELS] = inverse * (grad - shared - unit * along)


def first_step(
    flags, near_rows, far_rows, zonal, inner, weight_ref, state, gain, weight_in, weight_out,
    local, north, packed, mixture_out, field, *scratch, arrive, send, sent,
):
    edges(flags, near_rows, far_rows, local, north, *scratch, arrive)
    store_mixture(field, zonal, inner, scratch[0])

    @pl.loop(0, CELLS // CHUNK)
    def _(chunk):
        rows = pl.ds(pl.multiple_of(chunk * CHUNK, CHUNK), CHUNK)
        mixture = field[rows, 0:CHANNELS]
        mixture_out[rows] = mixture
        send(0, rows, chunk)
        normed = normalized(mixture, gain[...])[2]
        preact = jnp.dot(normed, weight_in[...], preferred_element_type=f32)
        hidden = (preact * gelu_parts(preact)[2]).astype(bf16)
        update = transposed_dot(hidden, weight_out[...])
        weight = weight_ref[rows].astype(f32)
        field[rows, 0:CHANNELS] = weight * (state[rows].astype(f32) + update)

    store_packed(field, packed)
    for chunk in range(CELLS // CHUNK):
        sent(0, slice(chunk * CHUNK, (chunk + 1) * CHUNK), chunk)


def second_step(
    flags, near_rows, far_rows, zonal, inner, weight_ref, cotangent, gain, weight_in, weight_out,
    local, north, packed, totals, normed, hidden, grad_preact, update, field, *scratch,
    arrive, send, sent,
):
    saved = normed, hidden, grad_preact, update
    edges(flags, near_rows, far_rows, local, north, *scratch, arrive)
    store_mixture(field, zonal, inner, scratch[0])

    @pl.loop(0, CELLS // CHUNK)
    def _(chunk):
        rows = pl.ds(pl.multiple_of(chunk * CHUNK, CHUNK), CHUNK)
        backward(
            rows,
            field[rows, 0:CHANNELS],
            cotangent[rows].astype(f32),
            weight_ref[rows].astype(f32),
            gain[...],
            weight_in,
            weight_out,
            field,
            saved,
        )

    store_totals(*saved, totals)
    send(0, slice(0, 2), 0)
    store_packed(field, packed)
    sent(0, slice(0, 2), 0)


def third_step(
    block_odd, flags, near_rows, far_rows, zonal, inner, weight_ref, cotangent, gain, weight_in, weight_out,
    local, north, mixture_in, before, packed, kept, sent_out, adjoint_out,
    totals, normed, hidden, grad_preact, update, field, *scratch, arrive, send, sent,
):
    saved = normed, hidden, grad_preact, update
    edges(flags, near_rows, far_rows, local, north, *scratch, arrive)
    store_mixture(field, zonal, inner, scratch[0])
    arrive(2)
    arrive(3)

    @pl.loop(0, CELLS // CHUNK)
    def _(chunk):
        rows = pl.ds(pl.multiple_of(chunk * CHUNK, CHUNK), CHUNK)
        weight = weight_ref[rows].astype(f32)
        adjoint = weight * cotangent[rows].astype(f32) + field[rows, 0:CHANNELS]
        adjoint_out[rows] = adjoint
        send(0, rows, chunk)
        backward(
            rows, mixture_in[rows], adjoint, weight, gain[...], weight_in, weight_out, field, saved
        )

    store_totals(*saved, totals, before)
    mine = block_odd[0]
    for k in range(4):
        rows = slice(k * 288, (k + 1) * 288)
        kept[k] = totals[mine, rows]
        sent_out[k] = totals[1 - mine, rows].astype(bf16)
    store_packed(field, packed)
    for chunk in range(CELLS // CHUNK):
        sent(0, slice(chunk * CHUNK, (chunk + 1) * CHUNK), chunk)


def last_step(
    flags, near_rows, far_rows, zonal, inner, weight_ref, local, north, adjoint, out, mark, *scratch,
    arrive,
):
    edges(flags, near_rows, far_rows, local, north, *scratch, arrive)
    arrive(2)
    mark[...] = jnp.zeros((8, 128), f32)
    for row in range(ROWS):
        cells = slice(row * WIDE, (row + 1) * WIDE)
        a, b = mixed_rows(row, zonal, inner, scratch[0])
        weight, value = weight_ref[cells].astype(f32), adjoint[cells]
        kept = weight * value
        out[row, :, 0:128] = (kept[:, :128] + a)[:COLS]
        out[row, :, 128:CHANNELS] = (kept[:, 128:] + b[:, : CHANNELS - 128])[:COLS]


def column_dot(left, right):
    return lax.dot_general(left, right, (((0,), (0,)), ((), ())), preferred_element_type=f32)


def store_totals(normed, hidden, grad_preact, update, out, before=None):
    for index, (left, right) in enumerate(((normed, grad_preact), (update, hidden))):
        product = column_dot(left[...], right[...])
        for k in range(HIDDEN // 128):
            rows = slice(k * CHANNELS, (k + 1) * CHANNELS)
            part = product[:, k * 128 : (k + 1) * 128]
            out[index, rows] = part if before is None else before[index, rows] + part


def packing(state, packed, field):
    for row in range(ROWS):
        field[row * WIDE : (row + 1) * WIDE, 0:CHANNELS] = state[
            row * WIDE : (row + 1) * WIDE
        ].astype(f32)
    store_packed(field, packed)


PARTS = [
    pltpu.VMEM((GROUPS, 64, TILE), f32),
    pltpu.VMEM((12, 48, 128), f32),
    pltpu.VMEM((GROUPS, 4, 48, 128), f32),
    pltpu.VMEM((64, 7 * TILE), bf16),
    pltpu.VMEM((14 * TILE, TILE), bf16),
]
FIELD = [pltpu.VMEM((CELLS, 256), f32)]


def shape(dims, dtype):
    return jax.ShapeDtypeStruct(dims, dtype)


def run(body, outs, scalars, args, scratch, name, us=1.0, after=(), late=(), far_outs=()):
    vmem, hbm = pl.BlockSpec(memory_space=pltpu.VMEM), pl.BlockSpec(memory_space=pltpu.HBM)
    sizes = [len(scalars), len(args), len(late), len(after), len(outs), len(far_outs)]
    sizes += [len(late), len(far_outs)]

    def called(*refs):
        groups, start = [], 0
        for size in sizes:
            groups.append(refs[start : start + size])
            start += size
        numbers, ins, sources, _, results, targets, fetched, staged = groups
        rest = refs[start:]
        options = {}
        if late:
            arrivals, rest = rest[0], rest[1:]
            copies = [
                pltpu.make_async_copy(source, place, arrivals.at[i])
                for i, (source, place) in enumerate(zip(sources, fetched))
            ]
            for copy in copies:
                copy.start()
            options["arrive"] = lambda i: copies[i].wait()
        if far_outs:
            departures, rest = rest[0], rest[1:]

            def leaving(i, rows, slot):
                return pltpu.make_async_copy(
                    staged[i].at[rows], targets[i].at[rows], departures.at[slot]
                )

            options["send"] = lambda i, rows, slot: leaving(i, rows, slot).start()
            options["sent"] = lambda i, rows, slot: leaving(i, rows, slot).wait()
        body(*numbers, *ins, *fetched, *results, *staged, *rest, **options)

    extra = [pltpu.VMEM(x.shape, x.dtype) for x in (*late, *far_outs)]
    if late:
        extra.append(pltpu.SemaphoreType.DMA((len(late),)))
    if far_outs:
        extra.append(pltpu.SemaphoreType.DMA((8,)))
    return pl.pallas_call(
        called,
        out_shape=[*outs, *far_outs],
        in_specs=[pl.BlockSpec(memory_space=pltpu.SMEM)] * len(scalars)
        + [vmem] * len(args)
        + [hbm] * len(late)
        + [pl.BlockSpec(memory_space=pl.ANY)] * len(after),
        out_specs=[vmem] * len(outs) + [hbm] * len(far_outs),
        scratch_shapes=extra + scratch,
        compiler_params=pltpu.CompilerParams(vmem_limit_bytes=VMEM_LIMIT),
        cost_estimate=pl.CostEstimate(
            flops=int(us * 1.1e9), bytes_accessed=int(us * 1e6), transcendentals=0
        ),
        name=name,
    )(*scalars, *args, *late, *after)


PACKED = [shape((48, WIDE, 128), bf16)]
SAVED = [
    pltpu.VMEM((CELLS, CHANNELS), bf16),
    pltpu.VMEM((CELLS, HIDDEN), bf16),
    pltpu.VMEM((CELLS, HIDDEN), bf16),
    pltpu.VMEM((CELLS, CHANNELS), bf16),
]


def flat_cells(block):
    padded = jnp.pad(block, ((0, 0), (0, WIDE - COLS), (0, 0)))
    return padded.reshape(CELLS, -1)


TOTALS = shape((2, HIDDEN // 128 * CHANNELS, 128), f32)
ZONAL = shape((GROUPS, CHUNK, TILE), f32)
RIMS = shape((6, 40, 128), bf16)
def filtered(packed, odds, rows, ready=()):
    block_odd, band_odd = odds
    near, far, local, north = rows
    inner, outer = block_swaps(packed)
    (zonal,) = run(
        near_body,
        [ZONAL],
        (block_odd,),
        (packed, inner),
        [
            pltpu.VMEM((48, 72, 128), f32),
            pltpu.VMEM((GROUPS, ROWS, 64, 128), f32),
            pltpu.VMEM((CHUNK, 16 * TILE), bf16),
            pltpu.VMEM((16 * TILE, TILE), bf16),
        ],
        "near_zonal",
        4.0,
        after=ready,
        late=(near,),
    )
    rims = run(
        rims_body,
        [RIMS] * 2,
        odds,
        (packed, inner, outer),
        [pltpu.VMEM((12, 40, 128), f32)],
        "rims",
        0.3,
        after=(zonal,),
    )
    marks = [zonal, rims[0]]
    near_rows, far_rows = rim_swaps(*rims)
    zonal, mixed = run(
        inner_body,
        [ZONAL, ZONAL],
        (block_odd,),
        (packed, inner, outer, zonal),
        [
            pltpu.VMEM((48, 48, 128), f32),
            pltpu.VMEM((GROUPS, ROWS, 40, 128), f32),
            pltpu.VMEM((48, 48, 128), f32),
            pltpu.VMEM((GROUPS, 16, 48, 128), f32),
            pltpu.VMEM((CHUNK, 8 * TILE), bf16),
            pltpu.VMEM((CHUNK, 7 * TILE), bf16),
            pltpu.VMEM((LOCAL_TILES * TILE, TILE), bf16),
        ],
        "inner_filters",
        5.0,
        late=(far, local),
    )
    return (near_rows, far_rows, zonal, mixed), (local, north), (*marks, mixed)


def shards(
    ocean_state, ocean_mask, cotangent, kernel, zonal_taps, norm_gain, weight_in, weight_out
):
    band = lax.axis_index("band")
    at_top = band == lax.axis_size("band") - 1
    block_odd = lax.axis_index("blk") % 2
    odds = (
        block_odd.astype(jnp.int32).reshape(1),
        jnp.stack([band % 2, (band == 0).astype(jnp.int32), at_top.astype(jnp.int32)]),
    )
    state = flat_cells(ocean_state)
    (packed,) = run(packing, PACKED, (), (state,), FIELD, "packing")
    weight = flat_cells(jnp.broadcast_to(ocean_mask[:, :, None].astype(bf16), ocean_state.shape))
    cells = flat_cells(cotangent)
    mlp = (norm_gain[None], weight_in, weight_out.T)
    zonal_forth = zonal_rows(zonal_taps, block_odd == 1)
    zonal_back = zonal_rows(zonal_taps[::-1], block_odd == 1)
    local_forth, local_back = local_rows(kernel), local_rows(kernel[::-1, ::-1])
    north_back = jnp.where(at_top, local_forth, local_back)
    forth = (*zonal_forth, local_forth, local_forth)
    back = (*zonal_back, local_back, north_back)
    parts, coefficients, _ = filtered(packed, odds, forth, (weight, *back))
    cell_array = shape((CELLS, CHANNELS), f32)
    packed, mixture = run(
        first_step,
        PACKED,
        odds[1:],
        (*parts, weight, state, *mlp),
        FIELD + PARTS,
        "first_step",
        5.0,
        late=coefficients,
        far_outs=[cell_array],
    )
    parts, coefficients, marks = filtered(packed, odds, forth, (cells,))
    packed, totals = run(
        second_step,
        PACKED,
        odds[1:],
        (*parts, weight, cells, *mlp),
        SAVED + FIELD + PARTS,
        "second_step",
        7.0,
        late=coefficients,
        far_outs=[TOTALS],
    )
    parts, coefficients, marks = filtered(packed, odds, back)
    packed, kept, sent, adjoint = run(
        third_step,
        PACKED + [shape((4, 288, 128), f32), shape((4, 288, 128), bf16)],
        odds,
        (*parts, weight, cells, *mlp),
        [pltpu.VMEM(TOTALS.shape, f32)] + SAVED + FIELD + PARTS,
        "third_step",
        7.0,
        late=(*coefficients, mixture, totals),
        far_outs=[cell_array],
    )
    parts, coefficients, marks = filtered(packed, odds, back)
    grad_state, final = run(
        last_step,
        [shape((ROWS, COLS, CHANNELS), f32), shape((8, 128), f32)],
        odds[1:],
        (*parts, weight),
        PARTS,
        "last_step",
        3.0,
        late=(*coefficients, adjoint),
    )
    own, other = summed(kept, sent, *marks, final)
    cell_count = ROWS * lax.axis_size("band") * COLS * lax.axis_size("blk")
    scaling = 1.0 / math.sqrt(cell_count)
    whole = shape((CHANNELS, HIDDEN), f32)

    def scaled(block_odd, own_ref, other_ref, in_out, out_out, sums):
        mine = block_odd[0]
        for k in range(4):
            rows = slice(k * 288, (k + 1) * 288)
            sums[mine, rows] = own_ref[k].astype(f32) * scaling
            sums[1 - mine, rows] = other_ref[k].astype(f32) * scaling
        for k in range(HIDDEN // 128):
            for out, index in ((in_out, 0), (out_out, 1)):
                out[:, k * 128 : (k + 1) * 128] = sums[index, k * CHANNELS : (k + 1) * CHANNELS]

    grad_in, grad_out = run(
        scaled,
        [whole, whole],
        odds[:1],
        (own, other),
        [pltpu.VMEM(TOTALS.shape, f32)],
        "scaled",
        0.5,
    )
    return (grad_state, grad_in, grad_out.T)


def solution(mesh):
    return jax.shard_map(
        shards,
        mesh=mesh,
        in_specs=(
            P("band", "blk", None),
            P("band", "blk"),
            P("band", "blk", None),
            P(),
            P(),
            P(),
            P(),
            P(),
        ),
        out_specs=(P("band", "blk", None), P(), P()),
        check_vma=False,
    )
```

```python
import math

import jax
import jax.numpy as jnp
from jax import lax
from jax.experimental import pallas as pl
from jax.experimental.pallas import tpu as pltpu
from jax.sharding import PartitionSpec as P

ROWS, COLS, CHANNELS, HIDDEN = 32, 30, 192, 768
WIDE = 32
CELLS = ROWS * WIDE
RIM, HALF, GROUP, GROUPS, PLACES = 3, 30, 64, 3, 4
ZONAL_TILES, LOCAL_TILES = 24, 21
TILE = GROUP * PLACES
CHUNK = 256
VMEM_LIMIT = 24 * 2**20
bf16, f32 = jnp.bfloat16, jnp.float32
epsilon = 1e-06
gelu_scale, gelu_cube = math.sqrt(2.0 / math.pi), 0.044715


def ways(axis, low, count):
    position = (lax.axis_index(axis) // low) % count
    pairs = [
        [(i, i ^ (low * step)) for i in range(lax.axis_size(axis))] for step in range(count)
    ]
    return position, pairs


def plus_body(*refs):
    total = refs[0][...].astype(f32)
    for ref in refs[1:-1]:
        total = total + ref[...].astype(f32)
    refs[-1][...] = total.astype(refs[-1].dtype)


def split_body(position, kept, arrived, own, first, second, third, total):
    total[...] = kept[...] + arrived[...].astype(f32)
    own[...] = total[position[0]]
    for step, out in ((1, first), (2, second), (3, third)):
        out[...] = total[position[0] ^ step].astype(bf16)


def join_body(position, own, first, second, third, out):
    for step, value in enumerate((own, first, second, third)):
        out[position[0] ^ step] = value[...]


def summed(kept, sent, zonal, rim, mixed, final, held):
    blocks = range(lax.axis_size("blk"))
    cores = [(i, i ^ 1) for i in blocks]
    position, pairs = ways("blk", 2, 4)
    position = position.astype(jnp.int32).reshape(1)
    piece, wide_piece = shape(sent.shape[1:], bf16), shape(sent.shape[1:], f32)
    arrived = lax.ppermute(sent, "blk", cores)
    own, *others = run(
        split_body,
        [wide_piece] + [piece] * 3,
        (position,),
        (kept, arrived),
        [pltpu.VMEM(kept.shape, f32)],
        "split",
        0.3,
        after=(held,),
    )
    others = [lax.ppermute(others[k - 1], "blk", pairs[k]) for k in (1, 2, 3)]
    (value,) = run(plus_body, [piece], (), (own, *others), [], "sum_y", 0.2, (zonal, held))
    stages = (
        ("blk", 8, (rim, held)),
        ("blk", 24, (held,)),
        ("band", 1, (mixed, held)),
        ("band", 2, (final,)),
        ("band", 6, ()),
    )
    for axis, step, after in stages:
        other = lax.ppermute(value, axis, [(i, i ^ step) for i in range(lax.axis_size(axis))])
        (value,) = run(plus_body, [piece], (), (value, other), [], f"sum_{axis}{step}", 0.2, after)
    others = [lax.ppermute(value, "blk", pairs[k]) for k in (1, 2, 3)]
    half = shape(sent.shape, bf16)
    (half,) = run(join_body, [half], (position,), (value, *others), [], "join", 0.2)
    return half, lax.ppermute(half, "blk", cores)


def block_swaps(packed):
    blocks = lax.axis_size("blk")
    inner = [(i, i ^ 1) for i in range(blocks)]
    outer = [(i, (i + 1) % blocks if i % 2 else (i - 1) % blocks) for i in range(blocks)]
    return lax.ppermute(packed, "blk", inner), lax.ppermute(packed, "blk", outer)


def rim_swaps(to_near, to_far):
    bands, blocks = lax.axis_size("band"), lax.axis_size("blk")
    near = [
        (b * blocks + i, (b ^ 1) * blocks + i) for b in range(bands) for i in range(blocks)
    ]
    far = [
        (b * blocks + i, (b + 1 if b % 2 else b - 1) * blocks + i)
        for b in range(1, bands - 1)
        for i in range(blocks)
    ]
    last = (bands - 1) * blocks
    far += [(last + i, last + blocks - 1 - i) for i in range(blocks)]
    far += [(i, i ^ 1) for i in range(blocks)]
    return (
        lax.ppermute(to_near, ("band", "blk"), near),
        lax.ppermute(to_far, ("band", "blk"), far),
    )


def zonal_rows(taps, odd_block):
    padded = jnp.pad(taps.astype(f32), ((24, 27), (0, 0))).reshape(-1, GROUPS, GROUP)
    padded = jnp.swapaxes(padded, 0, 1)
    padded = jnp.concatenate([padded, padded], axis=2)
    near = jnp.where(odd_block, padded[:, 0:88], padded[:, 23:111])
    far = jnp.where(odd_block, padded[:, 53:109], padded[:, 0:56])
    return near, far


def local_rows(kernel):
    padded = jnp.pad(kernel.astype(f32), ((4, 4), (0, 1), (0, 0)))
    padded = padded.reshape(15, 8, GROUPS, GROUP).transpose(2, 0, 1, 3)
    return jnp.concatenate([padded, padded], axis=3)


def low_lanes(shape):
    return lax.broadcasted_iota(jnp.int32, shape, len(shape) - 1) < GROUP


def swap_halves(value):
    return pltpu.roll(value, GROUP, value.ndim - 1)


def units():
    same = (
        lax.broadcasted_iota(jnp.int32, (GROUP, 128), 0)
        == lax.broadcasted_iota(jnp.int32, (GROUP, 128), 1) % GROUP
    )
    return jnp.where(same, 1.0, 0.0).astype(bf16)


def fill(out, unit, start, count, picks):
    low = low_lanes((8, 128))
    for half in range(2):
        rows = jnp.where(low, picks[2 * half], picks[2 * half + 1])
        for k in range(count):
            row = jnp.broadcast_to(rows[k : k + 1], (16, 128)).astype(bf16)
            block = jnp.concatenate([row] * (GROUP // 16)) * unit
            place = start + k * TILE
            out[place : place + GROUP, half * 128 : half * 128 + 128] = block


def zonal_matrix(out, unit, g, rows, count):
    for i in range(PLACES):
        for m in range(count // 8):
            base = [32 * m + 8 * (i - o) + 24 for o in range(PLACES)]
            fill(out, unit, m * 8 * TILE + i * GROUP, 8, [rows[g, k : k + 8] for k in base])


def local_matrix(out, unit, g, rows, blocks, start=0):
    for b in blocks:
        for i in range(PLACES):
            base = [4 * (b - 1) + i - o + RIM + 4 for o in range(PLACES)]
            fill(out, unit, start + i * GROUP, 7, [rows[g, k] for k in base])
        start += 7 * TILE


def pair_columns(wide, pairs, length):
    low = low_lanes((length, 128))
    for r in range(ROWS):
        value = wide[r, 0 : length + 8]
        turned = swap_halves(value)
        pairs[0, r] = jnp.where(low, value[:length], turned[8:])
        pairs[1, r] = jnp.where(low, turned[:length], value[8:])
    for r in range(16):
        value = wide[32 + r, 0 : length + 8]
        turned = swap_halves(value)
        pairs[2, r] = jnp.where(low, value[:length], turned[8:])
        pairs[2, 16 + r] = jnp.where(low, turned[:length], value[8:])


def zonal_product(g, pairs, left, rows, matrix, count):
    zonal_matrix(matrix, units(), g, rows, count)
    for tile in range(count):
        start = tile % 8 + 32 * (tile // 8)
        for half in range(2):
            value = pairs[g, :, start + 16 * half : start + 16 * half + 8, :]
            column = tile * TILE + half * 128
            left[:, column : column + 128] = value.reshape(CHUNK, 128).astype(bf16)
    return jnp.dot(left[...], matrix[0 : count * TILE], preferred_element_type=f32)


def near_body(block_odd, own, inner, rows, out, wide, pairs, left, matrix, arrive):
    odd = block_odd[0] == 1
    for r in range(48):
        wide[r, 0:8] = jnp.zeros((8, 128), f32)
        wide[r, 56:72] = jnp.zeros((16, 128), f32)

    @pl.when(odd)
    def _():
        for r in range(48):
            wide[r, 0:32] = inner[r].astype(f32)
            wide[r, 30:62] = own[r].astype(f32)

    @pl.when(jnp.logical_not(odd))
    def _():
        for r in range(48):
            wide[r, 7:39] = own[r].astype(f32)
            wide[r, 37:69] = inner[r].astype(f32)

    pair_columns(wide, pairs, 64)
    arrive(0)

    @pl.loop(0, GROUPS)
    def _(g):
        out[g] = zonal_product(g, pairs, left, rows, matrix, 16)


def rims_body(block_odd, flags, own, inner, outer, near_out, far_out, rim):
    odd, upper, top = block_odd[0] == 1, flags[0] == 1, flags[2] == 1
    places = list(range(3)) + list(range(32, 35)) + list(range(29, 32)) + list(range(45, 48))
    for k, r in enumerate(places):
        ins, outs = inner[r].astype(f32), outer[r].astype(f32)
        west, east = jnp.where(odd, ins, outs), jnp.where(odd, outs, ins)
        rim[k, 3:35] = own[r].astype(f32)
        rim[k, 0:3] = west[27:30]
        rim[k, 33:36] = east[0:3]
        rim[k, 36:40] = jnp.zeros((4, 128), f32)
    place = lax.broadcasted_iota(jnp.int32, (40, 40), 0)
    mirror = place + lax.broadcasted_iota(jnp.int32, (40, 40), 1) == COLS + 2 * RIM - 1
    mirror = jnp.where(mirror, 1.0, 0.0).astype(bf16)
    for k in range(6):
        low, high = rim[k], rim[6 + k]
        near_out[k] = jnp.where(upper, low, high).astype(bf16)
        far_out[k] = jnp.where(upper, high, low).astype(bf16)

    @pl.when(top)
    def _():
        for k in range(6):
            value = rim[8 - k] if k < 3 else swap_halves(rim[14 - k])
            turned = jnp.dot(mirror, value.astype(bf16), preferred_element_type=f32)
            far_out[k] = turned.astype(bf16)


def inner_body(
    block_odd, own, inner, outer, zonal, far, local, zonal_out, local_out,
    wide, pairs, field, row_pairs, zonal_left, local_left, matrix, arrive,
):
    odd = block_odd[0] == 1
    for r in range(48):
        wide[r] = jnp.zeros((48, 128), f32)

    @pl.when(odd)
    def _():
        for r in range(48):
            wide[r, 7:39] = outer[r].astype(f32)

    @pl.when(jnp.logical_not(odd))
    def _():
        for r in range(48):
            wide[r, 0:32] = outer[r].astype(f32)

    pair_columns(wide, pairs, 40)
    for r in range(48):
        ins, outs = inner[r].astype(f32), outer[r].astype(f32)
        west, east = jnp.where(odd, ins, outs), jnp.where(odd, outs, ins)
        field[r, 8:40] = own[r].astype(f32)
        field[r, 5:8] = west[27:30]
        field[r, 38:46] = east[0:8]
    low = low_lanes((48, 128))
    for q in range(16):
        first, second = field[2 * q], field[2 * q + 1]
        row_pairs[0, q] = jnp.where(low, first, swap_halves(second))
        row_pairs[1, q] = jnp.where(low, swap_halves(first), second)
        first, second = field[32 + 2 * q % 16], field[33 + 2 * q % 16]
        if q < 8:
            row_pairs[2, q] = jnp.where(low, first, swap_halves(second))
        else:
            row_pairs[2, q] = jnp.where(low, swap_halves(first), second)
    depth = 7 * TILE
    arrive(0)
    arrive(1)

    @pl.loop(0, GROUPS)
    def _(g):
        zonal_out[g] = zonal[g] + zonal_product(g, pairs, zonal_left, far, matrix, 8)
        local_matrix(matrix, units(), g, local, range(3))
        for shift in range(7):
            for half in range(2):
                column = shift * TILE + half * 128
                for block in range(8):
                    value = row_pairs[g, 2 * block + half, 5 + shift : 37 + shift, :]
                    local_left[block * 32 : block * 32 + 32, column : column + 128] = (
                        value.astype(bf16)
                    )
        local_out[g] = jnp.dot(
            local_left[...], matrix[depth : 2 * depth], preferred_element_type=f32
        )
        local_out[g, 32:256] += jnp.dot(
            local_left[0:224], matrix[0:depth], preferred_element_type=f32
        )
        local_out[g, 0:224] += jnp.dot(
            local_left[32:256], matrix[2 * depth : 3 * depth], preferred_element_type=f32
        )


def edges(band_odd, near_rows, far_rows, local, north, edge, rim, row_pairs, left, matrix, arrive):
    upper, bottom = band_odd[0] == 1, band_odd[1] == 1
    low = low_lanes((48, 128))
    nothing = jnp.zeros((48, 128), f32)
    for k in range(6):
        near, far = near_rows[k].astype(f32), far_rows[k].astype(f32)
        rim[k, 5:45] = jnp.where(upper, near, jnp.where(bottom, jnp.zeros_like(far), far))
        rim[6 + k, 5:45] = jnp.where(upper, far, near)
    below = [(nothing, nothing)] + [(rim[k], rim[3 + k]) for k in range(3)]
    above = [(rim[6 + k], rim[9 + k]) for k in range(3)] + [(nothing, nothing)]
    for side, rows in enumerate((below, above)):
        for half in range(2):
            (a, c), (b, d) = rows[2 * half], rows[2 * half + 1]
            place = 2 * side + half
            row_pairs[0, place] = jnp.where(low, a, swap_halves(b))
            row_pairs[1, place] = jnp.where(low, swap_halves(a), b)
            if side == 0:
                row_pairs[2, place] = jnp.where(low, swap_halves(c), d)
            else:
                row_pairs[2, place] = jnp.where(low, c, swap_halves(d))

    arrive(0)
    arrive(1)

    @pl.loop(0, GROUPS)
    def _(g):
        for side in range(2):
            for shift in range(7):
                for half in range(2):
                    column = shift * TILE + half * 128
                    value = row_pairs[g, 2 * side + half, 5 + shift : 37 + shift, :]
                    left[side * 32 : side * 32 + 32, column : column + 128] = value.astype(bf16)
        unit, depth = units(), 7 * TILE
        local_matrix(matrix, unit, g, local, (0,))
        local_matrix(matrix, unit, g, north, (2,), depth)
        edge[g, 0:32] = jnp.dot(left[0:32], matrix[0:depth], preferred_element_type=f32)
        edge[g, 32:64] = jnp.dot(
            left[32:64], matrix[depth : 2 * depth], preferred_element_type=f32
        )


def mixed_rows(row, zonal_out, local_out, edge):
    block, place = row // PLACES, row % PLACES

    def joined(first, second, third, odd):
        mask = low_lanes(first.shape)
        if odd:
            return jnp.where(mask, swap_halves(first), second), swap_halves(third)
        return jnp.where(mask, first, swap_halves(second)), third

    lanes = slice(place // 2 * 128, place // 2 * 128 + 128)
    parts = [local_out[g, block * 32 : block * 32 + 32, lanes] for g in range(GROUPS)]
    if block == 0:
        parts = [parts[g] + edge[g, 0:32, lanes] for g in range(GROUPS)]
    if block == ROWS // PLACES - 1:
        parts = [parts[g] + edge[g, 32:64, lanes] for g in range(GROUPS)]
    local_a, local_b = joined(*parts, place % 2)
    zonal_a, zonal_b = [], []
    for spot in range(PLACES):
        lanes = slice(spot // 2 * 128, spot // 2 * 128 + 128)
        parts = [zonal_out[g, row * 8 : row * 8 + 8, lanes] for g in range(GROUPS)]
        first, second = joined(*parts, spot % 2)
        zonal_a.append(first)
        zonal_b.append(second)
    zonal_a, zonal_b = jnp.concatenate(zonal_a), jnp.concatenate(zonal_b)
    a = local_a + zonal_a.astype(bf16).astype(f32)
    b = local_b + zonal_b.astype(bf16).astype(f32)
    return a, b


def store_mixture(mixture, *parts):
    for row in range(ROWS):
        a, b = mixed_rows(row, *parts)
        mixture[row * WIDE : (row + 1) * WIDE, 0:128] = a
        mixture[row * WIDE : (row + 1) * WIDE, 128:256] = b


def store_packed(field, packed):
    low = low_lanes((WIDE, 128))
    for row in range(ROWS):
        packed[row] = field[row * WIDE : (row + 1) * WIDE, 0:128].astype(bf16)
    for row in range(16):
        first = field[row * WIDE : (row + 1) * WIDE, 128:256]
        second = field[(row + 16) * WIDE : (row + 17) * WIDE, 128:256]
        packed[ROWS + row] = jnp.where(low, first, swap_halves(second)).astype(bf16)


def normalized(value, gain):
    average = jnp.mean(value, axis=-1, keepdims=True)
    centered = value - average
    variance = jnp.mean(centered * centered, axis=-1, keepdims=True)
    inverse = lax.rsqrt(variance + epsilon)
    unit = centered * inverse
    return unit, inverse, (unit * gain).astype(bf16)


def gelu_parts(value):
    square = value * value
    bent = jnp.tanh(value * (gelu_scale + gelu_scale * gelu_cube * square))
    share = 0.5 + 0.5 * bent
    return square, share, value * share


def transposed_dot(left, right):
    return lax.dot_general(left, right, (((1,), (1,)), ((), ())), preferred_element_type=f32)


def backward(rows, mixture, adjoint, weight, gain, weight_in, weight_out, field, saved):
    normed_out, hidden_out, preact_out, update_out = saved
    unit, inverse, normed = normalized(mixture, gain)
    preact = jnp.dot(normed, weight_in[...], preferred_element_type=f32)
    square, share, hidden = gelu_parts(preact)
    update = (weight * adjoint).astype(bf16)
    bend = 2.0 * gelu_scale + 6.0 * gelu_scale * gelu_cube * square
    slope = share * (1.0 + (preact - hidden) * bend)
    grad_preact = (jnp.dot(update, weight_out[...], preferred_element_type=f32) * slope).astype(bf16)
    normed_out[rows] = normed
    hidden_out[rows] = hidden.astype(bf16)
    preact_out[rows] = grad_preact
    update_out[rows] = update
    grad = transposed_dot(grad_preact, weight_in[...]) * gain
    shared = jnp.mean(grad, axis=-1, keepdims=True)
    along = jnp.mean(grad * unit, axis=-1, keepdims=True)
    field[rows, 0:CHANNELS] = inverse * (grad - shared - unit * along)


def first_step(
    flags, near_rows, far_rows, zonal, inner, weight_ref, state, gain, weight_in, weight_out,
    local, north, packed, mixture_out, field, *scratch, arrive, send, sent,
):
    edges(flags, near_rows, far_rows, local, north, *scratch, arrive)
    store_mixture(field, zonal, inner, scratch[0])

    @pl.loop(0, CELLS // CHUNK)
    def _(chunk):
        rows = pl.ds(pl.multiple_of(chunk * CHUNK, CHUNK), CHUNK)
        mixture = field[rows, 0:CHANNELS]
        mixture_out[rows] = mixture
        send(0, rows, chunk)
        normed = normalized(mixture, gain[...])[2]
        preact = jnp.dot(normed, weight_in[...], preferred_element_type=f32)
        hidden = gelu_parts(preact)[2].astype(bf16)
        update = transposed_dot(hidden, weight_out[...])
        weight = weight_ref[rows].astype(f32)
        field[rows, 0:CHANNELS] = weight * (state[rows].astype(f32) + update)

    store_packed(field, packed)
    for chunk in range(CELLS // CHUNK):
        sent(0, slice(chunk * CHUNK, (chunk + 1) * CHUNK), chunk)


def second_step(
    flags, near_rows, far_rows, zonal, inner, weight_ref, cotangent, gain, weight_in, weight_out,
    local, north, packed, totals, normed, hidden, grad_preact, update, field, *scratch,
    arrive, send, sent,
):
    saved = normed, hidden, grad_preact, update
    edges(flags, near_rows, far_rows, local, north, *scratch, arrive)
    store_mixture(field, zonal, inner, scratch[0])

    @pl.loop(0, CELLS // CHUNK)
    def _(chunk):
        rows = pl.ds(pl.multiple_of(chunk * CHUNK, CHUNK), CHUNK)
        backward(
            rows,
            field[rows, 0:CHANNELS],
            cotangent[rows].astype(f32),
            weight_ref[rows].astype(f32),
            gain[...],
            weight_in,
            weight_out,
            field,
            saved,
        )

    store_totals(*saved, totals)
    send(0, slice(0, 2), 0)
    store_packed(field, packed)
    sent(0, slice(0, 2), 0)


def third_step(
    block_odd, flags, near_rows, far_rows, zonal, inner, weight_ref, cotangent, gain, weight_in, weight_out,
    local, north, mixture_in, before, packed, kept, sent_out, adjoint_out,
    totals, normed, hidden, grad_preact, update, field, *scratch, arrive, send, sent,
):
    saved = normed, hidden, grad_preact, update
    edges(flags, near_rows, far_rows, local, north, *scratch, arrive)
    store_mixture(field, zonal, inner, scratch[0])
    arrive(2)
    arrive(3)

    @pl.loop(0, CELLS // CHUNK)
    def _(chunk):
        rows = pl.ds(pl.multiple_of(chunk * CHUNK, CHUNK), CHUNK)
        weight = weight_ref[rows].astype(f32)
        adjoint = weight * cotangent[rows].astype(f32) + field[rows, 0:CHANNELS]
        adjoint_out[rows] = adjoint
        send(0, rows, chunk)
        backward(
            rows, mixture_in[rows], adjoint, weight, gain[...], weight_in, weight_out, field, saved
        )

    store_totals(*saved, totals, before)
    mine = block_odd[0]
    for k in range(4):
        rows = slice(k * 288, (k + 1) * 288)
        kept[k] = totals[mine, rows]
        sent_out[k] = totals[1 - mine, rows].astype(bf16)
    store_packed(field, packed)
    for chunk in range(CELLS // CHUNK):
        sent(0, slice(chunk * CHUNK, (chunk + 1) * CHUNK), chunk)


def last_step(
    flags, near_rows, far_rows, zonal, inner, weight_ref, local, north, adjoint, out, mark, *scratch,
    arrive,
):
    edges(flags, near_rows, far_rows, local, north, *scratch, arrive)
    arrive(2)
    mark[...] = jnp.zeros((8, 128), f32)
    for row in range(ROWS):
        cells = slice(row * WIDE, (row + 1) * WIDE)
        a, b = mixed_rows(row, zonal, inner, scratch[0])
        weight, value = weight_ref[cells].astype(f32), adjoint[cells]
        kept = weight * value
        out[row, :, 0:128] = (kept[:, :128] + a)[:COLS]
        out[row, :, 128:CHANNELS] = (kept[:, 128:] + b[:, : CHANNELS - 128])[:COLS]


def column_dot(left, right):
    return lax.dot_general(left, right, (((0,), (0,)), ((), ())), preferred_element_type=f32)


def store_totals(normed, hidden, grad_preact, update, out, before=None):
    for index, (left, right) in enumerate(((normed, grad_preact), (update, hidden))):
        product = column_dot(left[...], right[...])
        for k in range(HIDDEN // 128):
            rows = slice(k * CHANNELS, (k + 1) * CHANNELS)
            part = product[:, k * 128 : (k + 1) * 128]
            out[index, rows] = part if before is None else before[index, rows] + part


def packing(state, packed, field):
    for row in range(ROWS):
        field[row * WIDE : (row + 1) * WIDE, 0:CHANNELS] = state[
            row * WIDE : (row + 1) * WIDE
        ].astype(f32)
    store_packed(field, packed)


PARTS = [
    pltpu.VMEM((GROUPS, 64, TILE), f32),
    pltpu.VMEM((12, 48, 128), f32),
    pltpu.VMEM((GROUPS, 4, 48, 128), f32),
    pltpu.VMEM((64, 7 * TILE), bf16),
    pltpu.VMEM((14 * TILE, TILE), bf16),
]
FIELD = [pltpu.VMEM((CELLS, 256), f32)]


def shape(dims, dtype):
    return jax.ShapeDtypeStruct(dims, dtype)


def run(body, outs, scalars, args, scratch, name, us=1.0, after=(), late=(), far_outs=()):
    vmem, hbm = pl.BlockSpec(memory_space=pltpu.VMEM), pl.BlockSpec(memory_space=pltpu.HBM)
    sizes = [len(scalars), len(args), len(late), len(after), len(outs), len(far_outs)]
    sizes += [len(late), len(far_outs)]

    def called(*refs):
        groups, start = [], 0
        for size in sizes:
            groups.append(refs[start : start + size])
            start += size
        numbers, ins, sources, _, results, targets, fetched, staged = groups
        rest = refs[start:]
        options = {}
        if late:
            arrivals, rest = rest[0], rest[1:]
            copies = [
                pltpu.make_async_copy(source, place, arrivals.at[i])
                for i, (source, place) in enumerate(zip(sources, fetched))
            ]
            for copy in copies:
                copy.start()
            options["arrive"] = lambda i: copies[i].wait()
        if far_outs:
            departures, rest = rest[0], rest[1:]

            def leaving(i, rows, slot):
                return pltpu.make_async_copy(
                    staged[i].at[rows], targets[i].at[rows], departures.at[slot]
                )

            options["send"] = lambda i, rows, slot: leaving(i, rows, slot).start()
            options["sent"] = lambda i, rows, slot: leaving(i, rows, slot).wait()
        body(*numbers, *ins, *fetched, *results, *staged, *rest, **options)

    extra = [pltpu.VMEM(x.shape, x.dtype) for x in (*late, *far_outs)]
    if late:
        extra.append(pltpu.SemaphoreType.DMA((len(late),)))
    if far_outs:
        extra.append(pltpu.SemaphoreType.DMA((8,)))
    return pl.pallas_call(
        called,
        out_shape=[*outs, *far_outs],
        in_specs=[pl.BlockSpec(memory_space=pltpu.SMEM)] * len(scalars)
        + [vmem] * len(args)
        + [hbm] * len(late)
        + [pl.BlockSpec(memory_space=pl.ANY)] * len(after),
        out_specs=[vmem] * len(outs) + [hbm] * len(far_outs),
        scratch_shapes=extra + scratch,
        compiler_params=pltpu.CompilerParams(vmem_limit_bytes=VMEM_LIMIT),
        cost_estimate=pl.CostEstimate(
            flops=int(us * 1.1e9), bytes_accessed=int(us * 1e6), transcendentals=0
        ),
        name=name,
    )(*scalars, *args, *late, *after)


PACKED = [shape((48, WIDE, 128), bf16)]
SAVED = [
    pltpu.VMEM((CELLS, CHANNELS), bf16),
    pltpu.VMEM((CELLS, HIDDEN), bf16),
    pltpu.VMEM((CELLS, HIDDEN), bf16),
    pltpu.VMEM((CELLS, CHANNELS), bf16),
]


def flat_cells(block):
    padded = jnp.pad(block, ((0, 0), (0, WIDE - COLS), (0, 0)))
    return padded.reshape(CELLS, -1)


TOTALS = shape((2, HIDDEN // 128 * CHANNELS, 128), f32)
ZONAL = shape((GROUPS, CHUNK, TILE), f32)
RIMS = shape((6, 40, 128), bf16)
def filtered(packed, odds, rows, ready=(), held=()):
    block_odd, band_odd = odds
    near, far, local, north = rows
    inner, outer = block_swaps(packed)
    (zonal,) = run(
        near_body,
        [ZONAL],
        (block_odd,),
        (packed, inner),
        [
            pltpu.VMEM((48, 72, 128), f32),
            pltpu.VMEM((GROUPS, ROWS, 64, 128), f32),
            pltpu.VMEM((CHUNK, 16 * TILE), bf16),
            pltpu.VMEM((16 * TILE, TILE), bf16),
        ],
        "near_zonal",
        4.0,
        after=(*ready, *held),
        late=(near,),
    )
    rims = run(
        rims_body,
        [RIMS] * 2,
        odds,
        (packed, inner, outer),
        [pltpu.VMEM((12, 40, 128), f32)],
        "rims",
        0.3,
        after=(zonal, *held),
    )
    marks = [zonal, rims[0]]
    near_rows, far_rows = rim_swaps(*rims)
    zonal, mixed = run(
        inner_body,
        [ZONAL, ZONAL],
        (block_odd,),
        (packed, inner, outer, zonal),
        [
            pltpu.VMEM((48, 48, 128), f32),
            pltpu.VMEM((GROUPS, ROWS, 40, 128), f32),
            pltpu.VMEM((48, 48, 128), f32),
            pltpu.VMEM((GROUPS, 16, 48, 128), f32),
            pltpu.VMEM((CHUNK, 8 * TILE), bf16),
            pltpu.VMEM((CHUNK, 7 * TILE), bf16),
            pltpu.VMEM((LOCAL_TILES * TILE, TILE), bf16),
        ],
        "inner_filters",
        5.0,
        after=held,
        late=(far, local),
    )
    return (near_rows, far_rows, zonal, mixed), (local, north), (*marks, mixed)


def shards(
    ocean_state, ocean_mask, cotangent, kernel, zonal_taps, norm_gain, weight_in, weight_out
):
    band = lax.axis_index("band")
    at_top = band == lax.axis_size("band") - 1
    block_odd = lax.axis_index("blk") % 2
    odds = (
        block_odd.astype(jnp.int32).reshape(1),
        jnp.stack([band % 2, (band == 0).astype(jnp.int32), at_top.astype(jnp.int32)]),
    )
    state = flat_cells(ocean_state)
    (packed,) = run(packing, PACKED, (), (state,), FIELD, "packing")
    weight = flat_cells(jnp.broadcast_to(ocean_mask[:, :, None].astype(bf16), ocean_state.shape))
    cells = flat_cells(cotangent)
    mlp = (norm_gain[None], weight_in, weight_out.T)
    zonal_forth = zonal_rows(zonal_taps, block_odd == 1)
    zonal_back = zonal_rows(zonal_taps[::-1], block_odd == 1)
    local_forth, local_back = local_rows(kernel), local_rows(kernel[::-1, ::-1])
    north_back = jnp.where(at_top, local_forth, local_back)
    forth = (*zonal_forth, local_forth, local_forth)
    back = (*zonal_back, local_back, north_back)
    parts, coefficients, _ = filtered(packed, odds, forth, (weight, *back))
    cell_array = shape((CELLS, CHANNELS), f32)
    packed, mixture = run(
        first_step,
        PACKED,
        odds[1:],
        (*parts, weight, state, *mlp),
        FIELD + PARTS,
        "first_step",
        5.0,
        late=coefficients,
        far_outs=[cell_array],
    )
    parts, coefficients, marks = filtered(packed, odds, forth, (cells,))
    packed, totals = run(
        second_step,
        PACKED,
        odds[1:],
        (*parts, weight, cells, *mlp),
        SAVED + FIELD + PARTS,
        "second_step",
        7.0,
        late=coefficients,
        far_outs=[TOTALS],
    )
    parts, coefficients, marks = filtered(packed, odds, back)
    packed, kept, sent, adjoint = run(
        third_step,
        PACKED + [shape((4, 288, 128), f32), shape((4, 288, 128), bf16)],
        odds,
        (*parts, weight, cells, *mlp),
        [pltpu.VMEM(TOTALS.shape, f32)] + SAVED + FIELD + PARTS,
        "third_step",
        7.0,
        late=(*coefficients, mixture, totals),
        far_outs=[cell_array],
    )
    parts, coefficients, marks = filtered(packed, odds, back, held=(adjoint,))
    grad_state, final = run(
        last_step,
        [shape((ROWS, COLS, CHANNELS), f32), shape((8, 128), f32)],
        odds[1:],
        (*parts, weight),
        PARTS,
        "last_step",
        3.0,
        late=(*coefficients, adjoint),
    )
    own, other = summed(kept, sent, *marks, final, adjoint)
    cell_count = ROWS * lax.axis_size("band") * COLS * lax.axis_size("blk")
    scaling = 1.0 / math.sqrt(cell_count)
    whole = shape((CHANNELS, HIDDEN), f32)

    def scaled(block_odd, own_ref, other_ref, in_out, out_out, sums):
        mine = block_odd[0]
        for k in range(4):
            rows = slice(k * 288, (k + 1) * 288)
            sums[mine, rows] = own_ref[k].astype(f32) * scaling
            sums[1 - mine, rows] = other_ref[k].astype(f32) * scaling
        for k in range(HIDDEN // 128):
            for out, index in ((in_out, 0), (out_out, 1)):
                out[:, k * 128 : (k + 1) * 128] = sums[index, k * CHANNELS : (k + 1) * CHANNELS]

    grad_in, grad_out = run(
        scaled,
        [whole, whole],
        odds[:1],
        (own, other),
        [pltpu.VMEM(TOTALS.shape, f32)],
        "scaled",
        0.5,
    )
    return (grad_state, grad_in, grad_out.T)


def solution(mesh):
    return jax.shard_map(
        shards,
        mesh=mesh,
        in_specs=(
            P("band", "blk", None),
            P("band", "blk"),
            P("band", "blk", None),
            P(),
            P(),
            P(),
            P(),
            P(),
        ),
        out_specs=(P("band", "blk", None), P(), P()),
        check_vma=False,
    )
```

```python
import math

import jax
import jax.numpy as jnp
from jax import lax
from jax.experimental import pallas as pl
from jax.experimental.pallas import tpu as pltpu
from jax.sharding import PartitionSpec as P

ROWS, COLS, CHANNELS, HIDDEN = 32, 30, 192, 768
WIDE = 32
CELLS = ROWS * WIDE
RIM, HALF, GROUP, GROUPS, PLACES = 3, 30, 64, 3, 4
ZONAL_TILES, LOCAL_TILES = 24, 21
TILE = GROUP * PLACES
CHUNK = 256
VMEM_LIMIT = 30 * 2**20
bf16, f32 = jnp.bfloat16, jnp.float32
epsilon = 1e-06
gelu_scale, gelu_cube = math.sqrt(2.0 / math.pi), 0.044715


def ways(axis, low, count):
    position = (lax.axis_index(axis) // low) % count
    pairs = [
        [(i, i ^ (low * step)) for i in range(lax.axis_size(axis))] for step in range(count)
    ]
    return position, pairs


def plus_body(*refs):
    total = refs[0][...].astype(f32)
    for ref in refs[1:-1]:
        total = total + ref[...].astype(f32)
    refs[-1][...] = total.astype(refs[-1].dtype)


def split_body(position, kept, arrived, own, first, second, third, total):
    total[...] = kept[...] + arrived[...].astype(f32)
    own[...] = total[position[0]]
    for step, out in ((1, first), (2, second), (3, third)):
        out[...] = total[position[0] ^ step].astype(bf16)


def join_body(position, own, first, second, third, out):
    for step, value in enumerate((own, first, second, third)):
        out[position[0] ^ step] = value[...]


def summed(kept, sent, zonal, rim, mixed, final, held):
    blocks = range(lax.axis_size("blk"))
    cores = [(i, i ^ 1) for i in blocks]
    position, pairs = ways("blk", 2, 4)
    position = position.astype(jnp.int32).reshape(1)
    piece, wide_piece = shape(sent.shape[1:], bf16), shape(sent.shape[1:], f32)
    arrived = lax.ppermute(sent, "blk", cores)
    own, *others = run(
        split_body,
        [wide_piece] + [piece] * 3,
        (position,),
        (kept, arrived),
        [pltpu.VMEM(kept.shape, f32)],
        "split",
        0.3,
        after=(held,),
    )
    others = [lax.ppermute(others[k - 1], "blk", pairs[k]) for k in (1, 2, 3)]
    (value,) = run(plus_body, [piece], (), (own, *others), [], "sum_y", 0.2, (zonal, held))
    stages = (
        ("blk", 8, (rim, held)),
        ("blk", 24, (held,)),
        ("band", 1, (mixed, held)),
        ("band", 2, (final,)),
        ("band", 6, ()),
    )
    for axis, step, after in stages:
        other = lax.ppermute(value, axis, [(i, i ^ step) for i in range(lax.axis_size(axis))])
        (value,) = run(plus_body, [piece], (), (value, other), [], f"sum_{axis}{step}", 0.2, after)
    others = [lax.ppermute(value, "blk", pairs[k]) for k in (1, 2, 3)]
    half = shape(sent.shape, bf16)
    (half,) = run(join_body, [half], (position,), (value, *others), [], "join", 0.2)
    return half, lax.ppermute(half, "blk", cores)


def block_swaps(packed):
    blocks = lax.axis_size("blk")
    inner = [(i, i ^ 1) for i in range(blocks)]
    outer = [(i, (i + 1) % blocks if i % 2 else (i - 1) % blocks) for i in range(blocks)]
    return lax.ppermute(packed, "blk", inner), lax.ppermute(packed, "blk", outer)


def rim_swaps(to_near, to_far):
    bands, blocks = lax.axis_size("band"), lax.axis_size("blk")
    near = [
        (b * blocks + i, (b ^ 1) * blocks + i) for b in range(bands) for i in range(blocks)
    ]
    far = [
        (b * blocks + i, (b + 1 if b % 2 else b - 1) * blocks + i)
        for b in range(1, bands - 1)
        for i in range(blocks)
    ]
    last = (bands - 1) * blocks
    far += [(last + i, last + blocks - 1 - i) for i in range(blocks)]
    far += [(i, i ^ 1) for i in range(blocks)]
    return (
        lax.ppermute(to_near, ("band", "blk"), near),
        lax.ppermute(to_far, ("band", "blk"), far),
    )


def zonal_rows(taps, odd_block):
    padded = jnp.pad(taps.astype(f32), ((24, 27), (0, 0))).reshape(-1, GROUPS, GROUP)
    padded = jnp.swapaxes(padded, 0, 1)
    padded = jnp.concatenate([padded, padded], axis=2)
    near = jnp.where(odd_block, padded[:, 0:88], padded[:, 23:111])
    far = jnp.where(odd_block, padded[:, 53:109], padded[:, 0:56])
    return near, far


def local_rows(kernel):
    padded = jnp.pad(kernel.astype(f32), ((4, 4), (0, 1), (0, 0)))
    padded = padded.reshape(15, 8, GROUPS, GROUP).transpose(2, 0, 1, 3)
    return jnp.concatenate([padded, padded], axis=3)


def low_lanes(shape):
    return lax.broadcasted_iota(jnp.int32, shape, len(shape) - 1) < GROUP


def swap_halves(value):
    return pltpu.roll(value, GROUP, value.ndim - 1)


def units():
    same = (
        lax.broadcasted_iota(jnp.int32, (GROUP, 128), 0)
        == lax.broadcasted_iota(jnp.int32, (GROUP, 128), 1) % GROUP
    )
    return jnp.where(same, 1.0, 0.0).astype(bf16)


def fill(out, unit, start, count, picks):
    low = low_lanes((8, 128))
    for half in range(2):
        rows = jnp.where(low, picks[2 * half], picks[2 * half + 1])
        for k in range(count):
            row = jnp.broadcast_to(rows[k : k + 1], (16, 128)).astype(bf16)
            block = jnp.concatenate([row] * (GROUP // 16)) * unit
            place = start + k * TILE
            out[place : place + GROUP, half * 128 : half * 128 + 128] = block


def zonal_matrix(out, unit, g, rows, count):
    for i in range(PLACES):
        for m in range(count // 8):
            base = [32 * m + 8 * (i - o) + 24 for o in range(PLACES)]
            fill(out, unit, m * 8 * TILE + i * GROUP, 8, [rows[g, k : k + 8] for k in base])


def local_matrix(out, unit, g, rows, blocks, start=0):
    for b in blocks:
        for i in range(PLACES):
            base = [4 * (b - 1) + i - o + RIM + 4 for o in range(PLACES)]
            fill(out, unit, start + i * GROUP, 7, [rows[g, k] for k in base])
        start += 7 * TILE


def pair_columns(wide, pairs, length):
    low = low_lanes((length, 128))
    for r in range(ROWS):
        value = wide[r, 0 : length + 8]
        turned = swap_halves(value)
        pairs[0, r] = jnp.where(low, value[:length], turned[8:])
        pairs[1, r] = jnp.where(low, turned[:length], value[8:])
    for r in range(16):
        value = wide[32 + r, 0 : length + 8]
        turned = swap_halves(value)
        pairs[2, r] = jnp.where(low, value[:length], turned[8:])
        pairs[2, 16 + r] = jnp.where(low, turned[:length], value[8:])


def zonal_product(g, pairs, left, rows, matrix, count):
    zonal_matrix(matrix, units(), g, rows, count)
    for tile in range(count):
        start = tile % 8 + 32 * (tile // 8)
        for half in range(2):
            value = pairs[g, :, start + 16 * half : start + 16 * half + 8, :]
            column = tile * TILE + half * 128
            left[:, column : column + 128] = value.reshape(CHUNK, 128).astype(bf16)
    return jnp.dot(left[...], matrix[0 : count * TILE], preferred_element_type=f32)


def near_body(block_odd, own, inner, rows, out, wide, pairs, left, matrix, arrive):
    odd = block_odd[0] == 1
    for r in range(48):
        wide[r, 0:8] = jnp.zeros((8, 128), f32)
        wide[r, 56:72] = jnp.zeros((16, 128), f32)

    @pl.when(odd)
    def _():
        for r in range(48):
            wide[r, 0:32] = inner[r].astype(f32)
            wide[r, 30:62] = own[r].astype(f32)

    @pl.when(jnp.logical_not(odd))
    def _():
        for r in range(48):
            wide[r, 7:39] = own[r].astype(f32)
            wide[r, 37:69] = inner[r].astype(f32)

    pair_columns(wide, pairs, 64)
    arrive(0)

    for g in range(GROUPS):
        out[g] = zonal_product(g, pairs, left.at[g % 2], rows, matrix.at[g % 2], 16)


def rims_body(block_odd, flags, own, inner, outer, near_out, far_out, rim):
    odd, upper, top = block_odd[0] == 1, flags[0] == 1, flags[2] == 1
    places = list(range(3)) + list(range(32, 35)) + list(range(29, 32)) + list(range(45, 48))
    for k, r in enumerate(places):
        ins, outs = inner[r].astype(f32), outer[r].astype(f32)
        west, east = jnp.where(odd, ins, outs), jnp.where(odd, outs, ins)
        rim[k, 3:35] = own[r].astype(f32)
        rim[k, 0:3] = west[27:30]
        rim[k, 33:36] = east[0:3]
        rim[k, 36:40] = jnp.zeros((4, 128), f32)
    place = lax.broadcasted_iota(jnp.int32, (40, 40), 0)
    mirror = place + lax.broadcasted_iota(jnp.int32, (40, 40), 1) == COLS + 2 * RIM - 1
    mirror = jnp.where(mirror, 1.0, 0.0).astype(bf16)
    for k in range(6):
        low, high = rim[k], rim[6 + k]
        near_out[k] = jnp.where(upper, low, high).astype(bf16)
        far_out[k] = jnp.where(upper, high, low).astype(bf16)

    @pl.when(top)
    def _():
        for k in range(6):
            value = rim[8 - k] if k < 3 else swap_halves(rim[14 - k])
            turned = jnp.dot(mirror, value.astype(bf16), preferred_element_type=f32)
            far_out[k] = turned.astype(bf16)


def inner_body(
    block_odd, own, inner, outer, zonal, far, local, zonal_out, local_out,
    wide, pairs, field, row_pairs, zonal_lefts, local_lefts, far_matrices, matrices, arrive,
):
    odd = block_odd[0] == 1
    for r in range(48):
        wide[r] = jnp.zeros((48, 128), f32)

    @pl.when(odd)
    def _():
        for r in range(48):
            wide[r, 7:39] = outer[r].astype(f32)

    @pl.when(jnp.logical_not(odd))
    def _():
        for r in range(48):
            wide[r, 0:32] = outer[r].astype(f32)

    pair_columns(wide, pairs, 40)
    for r in range(48):
        ins, outs = inner[r].astype(f32), outer[r].astype(f32)
        west, east = jnp.where(odd, ins, outs), jnp.where(odd, outs, ins)
        field[r, 8:40] = own[r].astype(f32)
        field[r, 5:8] = west[27:30]
        field[r, 38:46] = east[0:8]
    low = low_lanes((48, 128))
    for q in range(16):
        first, second = field[2 * q], field[2 * q + 1]
        row_pairs[0, q] = jnp.where(low, first, swap_halves(second))
        row_pairs[1, q] = jnp.where(low, swap_halves(first), second)
        first, second = field[32 + 2 * q % 16], field[33 + 2 * q % 16]
        if q < 8:
            row_pairs[2, q] = jnp.where(low, first, swap_halves(second))
        else:
            row_pairs[2, q] = jnp.where(low, swap_halves(first), second)
    depth = 7 * TILE
    arrive(0)
    arrive(1)

    for g in range(GROUPS):
        far_matrix, matrix = far_matrices.at[g % 2], matrices.at[g % 2]
        zonal_left, local_left = zonal_lefts.at[g % 2], local_lefts.at[g % 2]
        zonal_out[g] = zonal[g] + zonal_product(g, pairs, zonal_left, far, far_matrix, 8)
        local_matrix(matrix, units(), g, local, range(3))
        for shift in range(7):
            for half in range(2):
                column = shift * TILE + half * 128
                for block in range(8):
                    value = row_pairs[g, 2 * block + half, 5 + shift : 37 + shift, :]
                    local_left[block * 32 : block * 32 + 32, column : column + 128] = (
                        value.astype(bf16)
                    )
        local_out[g] = jnp.dot(
            local_left[...], matrix[depth : 2 * depth], preferred_element_type=f32
        )
        local_out[g, 32:256] += jnp.dot(
            local_left[0:224], matrix[0:depth], preferred_element_type=f32
        )
        local_out[g, 0:224] += jnp.dot(
            local_left[32:256], matrix[2 * depth : 3 * depth], preferred_element_type=f32
        )


def edges(band_odd, near_rows, far_rows, local, north, edge, rim, row_pairs, left, matrix, arrive):
    upper, bottom = band_odd[0] == 1, band_odd[1] == 1
    low = low_lanes((48, 128))
    nothing = jnp.zeros((48, 128), f32)
    for k in range(6):
        near, far = near_rows[k].astype(f32), far_rows[k].astype(f32)
        rim[k, 5:45] = jnp.where(upper, near, jnp.where(bottom, jnp.zeros_like(far), far))
        rim[6 + k, 5:45] = jnp.where(upper, far, near)
    below = [(nothing, nothing)] + [(rim[k], rim[3 + k]) for k in range(3)]
    above = [(rim[6 + k], rim[9 + k]) for k in range(3)] + [(nothing, nothing)]
    for side, rows in enumerate((below, above)):
        for half in range(2):
            (a, c), (b, d) = rows[2 * half], rows[2 * half + 1]
            place = 2 * side + half
            row_pairs[0, place] = jnp.where(low, a, swap_halves(b))
            row_pairs[1, place] = jnp.where(low, swap_halves(a), b)
            if side == 0:
                row_pairs[2, place] = jnp.where(low, swap_halves(c), d)
            else:
                row_pairs[2, place] = jnp.where(low, c, swap_halves(d))

    arrive(0)
    arrive(1)

    @pl.loop(0, GROUPS)
    def _(g):
        for side in range(2):
            for shift in range(7):
                for half in range(2):
                    column = shift * TILE + half * 128
                    value = row_pairs[g, 2 * side + half, 5 + shift : 37 + shift, :]
                    left[side * 32 : side * 32 + 32, column : column + 128] = value.astype(bf16)
        unit, depth = units(), 7 * TILE
        local_matrix(matrix, unit, g, local, (0,))
        local_matrix(matrix, unit, g, north, (2,), depth)
        edge[g, 0:32] = jnp.dot(left[0:32], matrix[0:depth], preferred_element_type=f32)
        edge[g, 32:64] = jnp.dot(
            left[32:64], matrix[depth : 2 * depth], preferred_element_type=f32
        )


def mixed_rows(row, zonal_out, local_out, edge):
    block, place = row // PLACES, row % PLACES

    def joined(first, second, third, odd):
        mask = low_lanes(first.shape)
        if odd:
            return jnp.where(mask, swap_halves(first), second), swap_halves(third)
        return jnp.where(mask, first, swap_halves(second)), third

    lanes = slice(place // 2 * 128, place // 2 * 128 + 128)
    parts = [local_out[g, block * 32 : block * 32 + 32, lanes] for g in range(GROUPS)]
    if block == 0:
        parts = [parts[g] + edge[g, 0:32, lanes] for g in range(GROUPS)]
    if block == ROWS // PLACES - 1:
        parts = [parts[g] + edge[g, 32:64, lanes] for g in range(GROUPS)]
    local_a, local_b = joined(*parts, place % 2)
    zonal_a, zonal_b = [], []
    for spot in range(PLACES):
        lanes = slice(spot // 2 * 128, spot // 2 * 128 + 128)
        parts = [zonal_out[g, row * 8 : row * 8 + 8, lanes] for g in range(GROUPS)]
        first, second = joined(*parts, spot % 2)
        zonal_a.append(first)
        zonal_b.append(second)
    zonal_a, zonal_b = jnp.concatenate(zonal_a), jnp.concatenate(zonal_b)
    a = local_a + zonal_a.astype(bf16).astype(f32)
    b = local_b + zonal_b.astype(bf16).astype(f32)
    return a, b


def store_mixture(mixture, *parts):
    for row in range(ROWS):
        a, b = mixed_rows(row, *parts)
        mixture[row * WIDE : (row + 1) * WIDE, 0:128] = a
        mixture[row * WIDE : (row + 1) * WIDE, 128:256] = b


def store_packed(field, packed):
    low = low_lanes((WIDE, 128))
    for row in range(ROWS):
        packed[row] = field[row * WIDE : (row + 1) * WIDE, 0:128].astype(bf16)
    for row in range(16):
        first = field[row * WIDE : (row + 1) * WIDE, 128:256]
        second = field[(row + 16) * WIDE : (row + 17) * WIDE, 128:256]
        packed[ROWS + row] = jnp.where(low, first, swap_halves(second)).astype(bf16)


def normalized(value, gain):
    average = jnp.mean(value, axis=-1, keepdims=True)
    centered = value - average
    variance = jnp.mean(centered * centered, axis=-1, keepdims=True)
    inverse = lax.rsqrt(variance + epsilon)
    unit = centered * inverse
    return unit, inverse, (unit * gain).astype(bf16)


def gelu_parts(value):
    square = value * value
    bent = jnp.tanh(value * (gelu_scale + gelu_scale * gelu_cube * square))
    share = 0.5 + 0.5 * bent
    return square, share, value * share


def transposed_dot(left, right):
    return lax.dot_general(left, right, (((1,), (1,)), ((), ())), preferred_element_type=f32)


def backward(rows, mixture, adjoint, weight, gain, weight_in, weight_out, field, saved):
    normed_out, hidden_out, preact_out, update_out = saved
    unit, inverse, normed = normalized(mixture, gain)
    preact = jnp.dot(normed, weight_in[...], preferred_element_type=f32)
    square, share, hidden = gelu_parts(preact)
    update = (weight * adjoint).astype(bf16)
    bend = 2.0 * gelu_scale + 6.0 * gelu_scale * gelu_cube * square
    slope = share * (1.0 + (preact - hidden) * bend)
    grad_preact = (jnp.dot(update, weight_out[...], preferred_element_type=f32) * slope).astype(bf16)
    normed_out[rows] = normed
    hidden_out[rows] = hidden.astype(bf16)
    preact_out[rows] = grad_preact
    update_out[rows] = update
    grad = transposed_dot(grad_preact, weight_in[...]) * gain
    shared = jnp.mean(grad, axis=-1, keepdims=True)
    along = jnp.mean(grad * unit, axis=-1, keepdims=True)
    field[rows, 0:CHANNELS] = inverse * (grad - shared - unit * along)


def first_step(
    flags, near_rows, far_rows, zonal, inner, weight_ref, state, gain, weight_in, weight_out,
    local, north, packed, mixture_out, field, *scratch, arrive, send, sent,
):
    edges(flags, near_rows, far_rows, local, north, *scratch, arrive)
    store_mixture(field, zonal, inner, scratch[0])

    @pl.loop(0, CELLS // CHUNK)
    def _(chunk):
        rows = pl.ds(pl.multiple_of(chunk * CHUNK, CHUNK), CHUNK)
        mixture = field[rows, 0:CHANNELS]
        mixture_out[rows] = mixture
        send(0, rows, chunk)
        normed = normalized(mixture, gain[...])[2]
        preact = jnp.dot(normed, weight_in[...], preferred_element_type=f32)
        hidden = gelu_parts(preact)[2].astype(bf16)
        update = transposed_dot(hidden, weight_out[...])
        weight = weight_ref[rows].astype(f32)
        field[rows, 0:CHANNELS] = weight * (state[rows].astype(f32) + update)

    store_packed(field, packed)
    for chunk in range(CELLS // CHUNK):
        sent(0, slice(chunk * CHUNK, (chunk + 1) * CHUNK), chunk)


def second_step(
    flags, near_rows, far_rows, zonal, inner, weight_ref, cotangent, gain, weight_in, weight_out,
    local, north, packed, totals, normed, hidden, grad_preact, update, field, *scratch,
    arrive, send, sent,
):
    saved = normed, hidden, grad_preact, update
    edges(flags, near_rows, far_rows, local, north, *scratch, arrive)
    store_mixture(field, zonal, inner, scratch[0])

    @pl.loop(0, CELLS // CHUNK)
    def _(chunk):
        rows = pl.ds(pl.multiple_of(chunk * CHUNK, CHUNK), CHUNK)
        backward(
            rows,
            field[rows, 0:CHANNELS],
            cotangent[rows].astype(f32),
            weight_ref[rows].astype(f32),
            gain[...],
            weight_in,
            weight_out,
            field,
            saved,
        )

    store_totals(*saved, totals)
    send(0, slice(0, 2), 0)
    store_packed(field, packed)
    sent(0, slice(0, 2), 0)


def third_step(
    block_odd, flags, near_rows, far_rows, zonal, inner, weight_ref, cotangent, gain, weight_in, weight_out,
    local, north, mixture_in, before, packed, kept, sent_out, adjoint_out,
    totals, normed, hidden, grad_preact, update, field, *scratch, arrive, send, sent,
):
    saved = normed, hidden, grad_preact, update
    edges(flags, near_rows, far_rows, local, north, *scratch, arrive)
    store_mixture(field, zonal, inner, scratch[0])
    arrive(2)
    arrive(3)

    @pl.loop(0, CELLS // CHUNK)
    def _(chunk):
        rows = pl.ds(pl.multiple_of(chunk * CHUNK, CHUNK), CHUNK)
        weight = weight_ref[rows].astype(f32)
        adjoint = weight * cotangent[rows].astype(f32) + field[rows, 0:CHANNELS]
        adjoint_out[rows] = adjoint
        send(0, rows, chunk)
        backward(
            rows, mixture_in[rows], adjoint, weight, gain[...], weight_in, weight_out, field, saved
        )

    store_totals(*saved, totals, before)
    mine = block_odd[0]
    for k in range(4):
        rows = slice(k * 288, (k + 1) * 288)
        kept[k] = totals[mine, rows]
        sent_out[k] = totals[1 - mine, rows].astype(bf16)
    store_packed(field, packed)
    for chunk in range(CELLS // CHUNK):
        sent(0, slice(chunk * CHUNK, (chunk + 1) * CHUNK), chunk)


def last_step(
    flags, near_rows, far_rows, zonal, inner, weight_ref, local, north, adjoint, out, mark, *scratch,
    arrive,
):
    edges(flags, near_rows, far_rows, local, north, *scratch, arrive)
    arrive(2)
    mark[...] = jnp.zeros((8, 128), f32)
    for row in range(ROWS):
        cells = slice(row * WIDE, (row + 1) * WIDE)
        a, b = mixed_rows(row, zonal, inner, scratch[0])
        weight, value = weight_ref[cells].astype(f32), adjoint[cells]
        kept = weight * value
        out[row, :, 0:128] = (kept[:, :128] + a)[:COLS]
        out[row, :, 128:CHANNELS] = (kept[:, 128:] + b[:, : CHANNELS - 128])[:COLS]


def column_dot(left, right):
    return lax.dot_general(left, right, (((0,), (0,)), ((), ())), preferred_element_type=f32)


def store_totals(normed, hidden, grad_preact, update, out, before=None):
    for index, (left, right) in enumerate(((normed, grad_preact), (update, hidden))):
        product = column_dot(left[...], right[...])
        for k in range(HIDDEN // 128):
            rows = slice(k * CHANNELS, (k + 1) * CHANNELS)
            part = product[:, k * 128 : (k + 1) * 128]
            out[index, rows] = part if before is None else before[index, rows] + part


def packing(state, packed, field):
    for row in range(ROWS):
        field[row * WIDE : (row + 1) * WIDE, 0:CHANNELS] = state[
            row * WIDE : (row + 1) * WIDE
        ].astype(f32)
    store_packed(field, packed)


PARTS = [
    pltpu.VMEM((GROUPS, 64, TILE), f32),
    pltpu.VMEM((12, 48, 128), f32),
    pltpu.VMEM((GROUPS, 4, 48, 128), f32),
    pltpu.VMEM((64, 7 * TILE), bf16),
    pltpu.VMEM((14 * TILE, TILE), bf16),
]
FIELD = [pltpu.VMEM((CELLS, 256), f32)]


def shape(dims, dtype):
    return jax.ShapeDtypeStruct(dims, dtype)


def run(body, outs, scalars, args, scratch, name, us=1.0, after=(), late=(), far_outs=()):
    vmem, hbm = pl.BlockSpec(memory_space=pltpu.VMEM), pl.BlockSpec(memory_space=pltpu.HBM)
    sizes = [len(scalars), len(args), len(late), len(after), len(outs), len(far_outs)]
    sizes += [len(late), len(far_outs)]

    def called(*refs):
        groups, start = [], 0
        for size in sizes:
            groups.append(refs[start : start + size])
            start += size
        numbers, ins, sources, _, results, targets, fetched, staged = groups
        rest = refs[start:]
        options = {}
        if late:
            arrivals, rest = rest[0], rest[1:]
            copies = [
                pltpu.make_async_copy(source, place, arrivals.at[i])
                for i, (source, place) in enumerate(zip(sources, fetched))
            ]
            for copy in copies:
                copy.start()
            options["arrive"] = lambda i: copies[i].wait()
        if far_outs:
            departures, rest = rest[0], rest[1:]

            def leaving(i, rows, slot):
                return pltpu.make_async_copy(
                    staged[i].at[rows], targets[i].at[rows], departures.at[slot]
                )

            options["send"] = lambda i, rows, slot: leaving(i, rows, slot).start()
            options["sent"] = lambda i, rows, slot: leaving(i, rows, slot).wait()
        body(*numbers, *ins, *fetched, *results, *staged, *rest, **options)

    extra = [pltpu.VMEM(x.shape, x.dtype) for x in (*late, *far_outs)]
    if late:
        extra.append(pltpu.SemaphoreType.DMA((len(late),)))
    if far_outs:
        extra.append(pltpu.SemaphoreType.DMA((8,)))
    return pl.pallas_call(
        called,
        out_shape=[*outs, *far_outs],
        in_specs=[pl.BlockSpec(memory_space=pltpu.SMEM)] * len(scalars)
        + [vmem] * len(args)
        + [hbm] * len(late)
        + [pl.BlockSpec(memory_space=pl.ANY)] * len(after),
        out_specs=[vmem] * len(outs) + [hbm] * len(far_outs),
        scratch_shapes=extra + scratch,
        compiler_params=pltpu.CompilerParams(vmem_limit_bytes=VMEM_LIMIT),
        cost_estimate=pl.CostEstimate(
            flops=int(us * 1.1e9), bytes_accessed=int(us * 1e6), transcendentals=0
        ),
        name=name,
    )(*scalars, *args, *late, *after)


PACKED = [shape((48, WIDE, 128), bf16)]
SAVED = [
    pltpu.VMEM((CELLS, CHANNELS), bf16),
    pltpu.VMEM((CELLS, HIDDEN), bf16),
    pltpu.VMEM((CELLS, HIDDEN), bf16),
    pltpu.VMEM((CELLS, CHANNELS), bf16),
]


def flat_cells(block):
    padded = jnp.pad(block, ((0, 0), (0, WIDE - COLS), (0, 0)))
    return padded.reshape(CELLS, -1)


TOTALS = shape((2, HIDDEN // 128 * CHANNELS, 128), f32)
ZONAL = shape((GROUPS, CHUNK, TILE), f32)
RIMS = shape((6, 40, 128), bf16)
def filtered(packed, odds, rows, ready=(), held=()):
    block_odd, band_odd = odds
    near, far, local, north = rows
    inner, outer = block_swaps(packed)
    (zonal,) = run(
        near_body,
        [ZONAL],
        (block_odd,),
        (packed, inner),
        [
            pltpu.VMEM((48, 72, 128), f32),
            pltpu.VMEM((GROUPS, ROWS, 64, 128), f32),
            pltpu.VMEM((2, CHUNK, 16 * TILE), bf16),
            pltpu.VMEM((2, 16 * TILE, TILE), bf16),
        ],
        "near_zonal",
        4.0,
        after=(*ready, *held),
        late=(near,),
    )
    rims = run(
        rims_body,
        [RIMS] * 2,
        odds,
        (packed, inner, outer),
        [pltpu.VMEM((12, 40, 128), f32)],
        "rims",
        0.3,
        after=(zonal, *held),
    )
    marks = [zonal, rims[0]]
    near_rows, far_rows = rim_swaps(*rims)
    zonal, mixed = run(
        inner_body,
        [ZONAL, ZONAL],
        (block_odd,),
        (packed, inner, outer, zonal),
        [
            pltpu.VMEM((48, 48, 128), f32),
            pltpu.VMEM((GROUPS, ROWS, 40, 128), f32),
            pltpu.VMEM((48, 48, 128), f32),
            pltpu.VMEM((GROUPS, 16, 48, 128), f32),
            pltpu.VMEM((2, CHUNK, 8 * TILE), bf16),
            pltpu.VMEM((2, CHUNK, 7 * TILE), bf16),
            pltpu.VMEM((2, 8 * TILE, TILE), bf16),
            pltpu.VMEM((2, LOCAL_TILES * TILE, TILE), bf16),
        ],
        "inner_filters",
        5.0,
        after=held,
        late=(far, local),
    )
    return (near_rows, far_rows, zonal, mixed), (local, north), (*marks, mixed)


def shards(
    ocean_state, ocean_mask, cotangent, kernel, zonal_taps, norm_gain, weight_in, weight_out
):
    band = lax.axis_index("band")
    at_top = band == lax.axis_size("band") - 1
    block_odd = lax.axis_index("blk") % 2
    odds = (
        block_odd.astype(jnp.int32).reshape(1),
        jnp.stack([band % 2, (band == 0).astype(jnp.int32), at_top.astype(jnp.int32)]),
    )
    state = flat_cells(ocean_state)
    (packed,) = run(packing, PACKED, (), (state,), FIELD, "packing")
    weight = flat_cells(jnp.broadcast_to(ocean_mask[:, :, None].astype(bf16), ocean_state.shape))
    cells = flat_cells(cotangent)
    mlp = (norm_gain[None], weight_in, weight_out.T)
    zonal_forth = zonal_rows(zonal_taps, block_odd == 1)
    zonal_back = zonal_rows(zonal_taps[::-1], block_odd == 1)
    local_forth, local_back = local_rows(kernel), local_rows(kernel[::-1, ::-1])
    north_back = jnp.where(at_top, local_forth, local_back)
    forth = (*zonal_forth, local_forth, local_forth)
    back = (*zonal_back, local_back, north_back)
    parts, coefficients, _ = filtered(packed, odds, forth, (weight, *back))
    cell_array = shape((CELLS, CHANNELS), f32)
    packed, mixture = run(
        first_step,
        PACKED,
        odds[1:],
        (*parts, weight, state, *mlp),
        FIELD + PARTS,
        "first_step",
        5.0,
        late=coefficients,
        far_outs=[cell_array],
    )
    parts, coefficients, marks = filtered(packed, odds, forth, (cells,))
    packed, totals = run(
        second_step,
        PACKED,
        odds[1:],
        (*parts, weight, cells, *mlp),
        SAVED + FIELD + PARTS,
        "second_step",
        7.0,
        late=coefficients,
        far_outs=[TOTALS],
    )
    parts, coefficients, marks = filtered(packed, odds, back)
    packed, kept, sent, adjoint = run(
        third_step,
        PACKED + [shape((4, 288, 128), f32), shape((4, 288, 128), bf16)],
        odds,
        (*parts, weight, cells, *mlp),
        [pltpu.VMEM(TOTALS.shape, f32)] + SAVED + FIELD + PARTS,
        "third_step",
        7.0,
        late=(*coefficients, mixture, totals),
        far_outs=[cell_array],
    )
    parts, coefficients, marks = filtered(packed, odds, back, held=(adjoint,))
    grad_state, final = run(
        last_step,
        [shape((ROWS, COLS, CHANNELS), f32), shape((8, 128), f32)],
        odds[1:],
        (*parts, weight),
        PARTS,
        "last_step",
        3.0,
        late=(*coefficients, adjoint),
    )
    own, other = summed(kept, sent, *marks, final, adjoint)
    cell_count = ROWS * lax.axis_size("band") * COLS * lax.axis_size("blk")
    scaling = 1.0 / math.sqrt(cell_count)
    whole = shape((CHANNELS, HIDDEN), f32)

    def scaled(block_odd, own_ref, other_ref, in_out, out_out, sums):
        mine = block_odd[0]
        for k in range(4):
            rows = slice(k * 288, (k + 1) * 288)
            sums[mine, rows] = own_ref[k].astype(f32) * scaling
            sums[1 - mine, rows] = other_ref[k].astype(f32) * scaling
        for k in range(HIDDEN // 128):
            for out, index in ((in_out, 0), (out_out, 1)):
                out[:, k * 128 : (k + 1) * 128] = sums[index, k * CHANNELS : (k + 1) * CHANNELS]

    grad_in, grad_out = run(
        scaled,
        [whole, whole],
        odds[:1],
        (own, other),
        [pltpu.VMEM(TOTALS.shape, f32)],
        "scaled",
        0.5,
    )
    return (grad_state, grad_in, grad_out.T)


def solution(mesh):
    return jax.shard_map(
        shards,
        mesh=mesh,
        in_specs=(
            P("band", "blk", None),
            P("band", "blk"),
            P("band", "blk", None),
            P(),
            P(),
            P(),
            P(),
            P(),
        ),
        out_specs=(P("band", "blk", None), P(), P()),
        check_vma=False,
    )
```
